32 devices in a mesh: row: 4 (over z), ma: 8 (over y, x, core).
Axes of the slice: x: 2, y: 2, z: 4, core: 2. Of those that a mesh axis runs over, the one named last changes fastest.
Arguments:
- spectra: float32 [4, 2, 128, 4224], P(None, None, 'row', 'ma'), may hold values from -6 to 6
- dtheta_table: bfloat16 [4224, 768], P('ma'), may hold values from -0.046875 to 0.046875
- dphi_table: bfloat16 [4224, 768], P('ma'), may hold values from -0.046875 to 0.046875
- analysis_table: bfloat16 [4224, 768], P('ma'), may hold values from -6 to 6
- pair_index: int32 [8], replicated, may hold values from 0 to 255, as said below
- diffusivity: float32 [4], replicated, may hold values from 0.0001 to 0.0004
Outputs:
- new_spectra: float32 [4, 2, 128, 4224], P(None, None, 'row', 'ma')
The draws below stay inside these ranges and needn't reach their ends.
Inputs may be any that keep to these rules, and one draw needn't show every extreme that they name: 8 distinct values, among them always both 0 and the largest; position g holds the orders pair_index[g] and 511 - pair_index[g].
All inputs are finite; a program needn't handle non-finite values.
Results may differ from the reference program's by a relative error of at most 0.0057.
Values may be sent and summed in bfloat16 or wider, within the bound.
A program may use at most 64 MiB of HBM per device.

```python
import math
import jax
import jax.numpy as jnp
from jax import lax

LMAX = 511
NTH = 768
NPHI = 1536
SLOTS = 528
NR = 128
NPAIRS = 8


def draw_pair_index(key, part):
    half_count = (LMAX + 1) // 2
    first_key, second_key = jax.random.split(key)
    middle = jax.random.permutation(first_key, half_count - 2)[:NPAIRS - 2].astype(jnp.int32) + 1
    ends = jnp.array([0, half_count - 1], dtype=jnp.int32)
    values = jnp.concatenate([ends, middle])
    return jax.random.permutation(second_key, values).astype(jnp.int32)


def level_of(own_key, extent, cuts, least, largest):
    gain = 1.0
    for axis_at, parts in cuts:
        heights = jax.random.uniform(jax.random.fold_in(jax.random.fold_in(own_key, 6), axis_at), (parts,), jnp.float32, least / len(cuts), largest / len(cuts))
        gain = gain * jnp.repeat(jnp.exp(heights), extent[axis_at] // parts).reshape((-1,) + (1,) * (len(extent) - 1 - axis_at))
    return gain


def centred(rng, dims, deviation, bound, cuts=(), held_as=jnp.bfloat16):
    loudness = level_of(rng, dims, cuts, -0.22, 0.18) if cuts else 1.0
    drawn = jax.random.normal(rng, dims, jnp.float32) * deviation * loudness
    return jnp.minimum(jnp.maximum(drawn, -bound), bound).astype(held_as)


def setup_inputs(seed: int = 0) -> dict:
    arg_keys = jax.random.split(jax.random.key(seed), 7)
    return {
        "spectra": centred(arg_keys[0], (4, 2, NR, NPAIRS * SLOTS), 1.0, 6.0, ((2, 4), (3, 8)), jnp.float32),
        "dtheta_table": centred(arg_keys[1], (NPAIRS * SLOTS, NTH), (4 * NPAIRS * (LMAX + 1)) ** -0.5, 0.046875, ((0, 8),)),
        "dphi_table": centred(arg_keys[2], (NPAIRS * SLOTS, NTH), (4 * NPAIRS * (LMAX + 1)) ** -0.5, 0.046875, ((0, 8),)),
        "analysis_table": centred(arg_keys[3], (NPAIRS * SLOTS, NTH), 1.0, 6.0, ((0, 8),)),
        "pair_index": draw_pair_index(jax.random.fold_in(arg_keys[6], 71), 0),
        "diffusivity": jnp.clip(jnp.exp(jax.random.uniform(arg_keys[5], (4,), jnp.float32, math.log(0.0001), math.log(0.0004))), 0.0001, 0.0004),
    }


ROTATION = 2.0
SHELL_RADIUS = 16.0

def slot_layout(pair_values):
    slot_index = jnp.arange(SLOTS, dtype=jnp.int32)[None, :]
    lowest = pair_values.astype(jnp.int32)[:, None]
    first_part = slot_index < LMAX + 1 - lowest
    second_part = jnp.logical_and(jnp.logical_not(first_part), slot_index < LMAX + 2)
    degree = jnp.where(first_part, lowest + slot_index, slot_index - 1)
    wave_order = jnp.where(first_part, lowest, LMAX - lowest)
    return (first_part, second_part, degree, wave_order)

def fourier_tables(pair_values):
    lowest = pair_values.astype(jnp.int32)
    orders = jnp.stack([lowest, LMAX - lowest], axis=1)
    angle_step = jnp.arange(NPHI, dtype=jnp.int32)
    phases = orders[:, :, None] * angle_step[None, None, :] % NPHI
    angles = phases.astype(jnp.float32) * (2.0 * math.pi / NPHI)
    weight_order = jnp.where(orders == 0, 1.0, 2.0).astype(jnp.float32)[:, :, None]
    cosine = jnp.cos(angles)
    sine_part = jnp.sin(angles)
    synthesis = jnp.stack([weight_order * cosine, -weight_order * sine_part]).astype(jnp.bfloat16)
    analysis_fourier = (jnp.stack([cosine, -sine_part]) / NPHI).astype(jnp.bfloat16)
    return (synthesis, analysis_fourier)

def grid_products(grid_values):
    stream_theta, stream_phi, poloidal_theta, poloidal_phi = (grid_values[0], grid_values[1], grid_values[2], grid_values[3])
    thermal_theta, thermal_phi, magnetic_theta, magnetic_phi = (grid_values[4], grid_values[5], grid_values[6], grid_values[7])
    flow_theta = poloidal_theta - stream_phi
    flow_phi = poloidal_phi + stream_theta
    field_theta = -magnetic_phi
    field_phi = magnetic_theta
    stress = field_theta * field_phi - flow_theta * flow_phi
    pressure = 0.5 * (field_phi * field_phi - field_theta * field_theta) - 0.5 * (flow_phi * flow_phi - flow_theta * flow_theta)
    heat_flux = -(flow_theta * thermal_theta + flow_phi * thermal_phi)
    induction = -(flow_theta * field_phi - flow_phi * field_theta)
    return jnp.stack([stress, pressure, heat_flux, induction])

def coupled(source, partner, parity, degree, wave_order, alive):
    degree_real = degree.astype(jnp.float32)
    order_real = wave_order.astype(jnp.float32)
    lower_coupling = jnp.sqrt((degree_real * degree_real - order_real * order_real) * alive / jnp.maximum(4.0 * degree_real * degree_real - 1.0, 1.0))
    upper_degree = degree_real + 1.0
    upper_coupling = jnp.sqrt((upper_degree * upper_degree - order_real * order_real) / (4.0 * upper_degree * upper_degree - 1.0)) * alive * (degree < LMAX).astype(jnp.float32)
    spin_term = order_real / (degree_real * (degree_real + 1.0) + 2.0)
    turned = jnp.stack([-source[1], source[0]])
    below_slot = jnp.concatenate([jnp.zeros_like(partner[..., :1]), partner[..., :-1]], axis=-1)
    above_slot = jnp.concatenate([partner[..., 1:], jnp.zeros_like(partner[..., :1])], axis=-1)
    return ROTATION * (spin_term * turned + parity * (lower_coupling * below_slot + upper_coupling * above_slot))

def radial_solve(right_side, degree_flat, diffusivity):
    points = right_side.shape[2]
    counter = jnp.arange(1, points + 1, dtype=jnp.int32)
    product = counter[:, None] * counter[None, :] % (2 * (points + 1))
    sine_basis = math.sqrt(2.0 / (points + 1)) * jnp.sin(product.astype(jnp.float32) * (math.pi / (points + 1)))
    eigenvalues = 4.0 * (points + 1) * (points + 1) * jnp.sin(counter.astype(jnp.float32) * (math.pi / (2 * (points + 1)))) ** 2
    degree_real = degree_flat.astype(jnp.float32)
    horizontal = degree_real * (degree_real + 1.0) / (SHELL_RADIUS * SHELL_RADIUS)
    modal_part = jnp.einsum('jk,fcks->fcjs', sine_basis, right_side, precision=lax.Precision.HIGHEST)
    factor = 1.0 + diffusivity[:, None, None, None] * (eigenvalues[None, None, :, None] + horizontal[None, None, None, :])
    return jnp.einsum('jk,fcks->fcjs', sine_basis, modal_part / factor, precision=lax.Precision.HIGHEST)

def reference(spectra, dtheta_table, dphi_table, analysis_table, pair_index, diffusivity):
    first_part, second_part, degree, wave_order = slot_layout(pair_index)
    alive = jnp.logical_or(first_part, second_part).astype(jnp.float32)
    part_masks = jnp.stack([first_part, second_part], axis=1).astype(jnp.float32)
    masked_state = spectra.reshape(4, 2, NR, NPAIRS, SLOTS) * alive
    coeffs = masked_state.astype(jnp.bfloat16)
    spread = coeffs.astype(jnp.float32)[:, :, :, :, None, :] * part_masks[None, None, None]
    theta_rows = dtheta_table.reshape(NPAIRS, SLOTS, NTH).astype(jnp.float32)
    phi_rows = dphi_table.reshape(NPAIRS, SLOTS, NTH).astype(jnp.float32)
    along_theta = jnp.einsum('fcrpjs,pst->fcrpjt', spread, theta_rows)
    phi_direct = jnp.einsum('fcrpjs,pst->fcrpjt', spread, phi_rows)
    along_phi = jnp.stack([-phi_direct[:, 1], phi_direct[:, 0]], axis=1)
    grid_spectra = jnp.stack([along_theta, along_phi], axis=1)
    grid_spectra = jnp.transpose(grid_spectra, (3, 0, 1, 2, 4, 5, 6)).reshape(NR, 8, 2, NPAIRS, 2, NTH).astype(jnp.bfloat16)
    synthesis, analysis_fourier = fourier_tables(pair_index)
    synthesis_real = synthesis.astype(jnp.float32)
    analysis_real = analysis_fourier.astype(jnp.float32)

    def one_radius(radius_block):
        grid_values = jnp.einsum('qcpjt,cpjk->qtk', radius_block.astype(jnp.float32), synthesis_real)
        products = grid_products(grid_values).astype(jnp.bfloat16)
        return jnp.einsum('ftk,cpjk->fcpjt', products.astype(jnp.float32), analysis_real).astype(jnp.bfloat16)
    returned = lax.map(one_radius, grid_spectra)
    analysis_rows = analysis_table.reshape(NPAIRS, SLOTS, NTH).astype(jnp.float32)
    projected = jnp.einsum('rfcpjt,pst->fcrpjs', returned.astype(jnp.float32), analysis_rows)
    nonlinear = lax.optimization_barrier(jnp.sum(projected * part_masks[None, None, None], axis=4))
    forcing = jnp.stack([coupled(masked_state[0], masked_state[1], 1.0, degree, wave_order, alive), coupled(masked_state[1], masked_state[0], -1.0, degree, wave_order, alive)])
    forcing = jnp.concatenate([forcing, jnp.zeros_like(forcing)], axis=0)
    right_side = (masked_state + nonlinear + forcing) * alive
    solved = radial_solve(right_side.reshape(4, 2, NR, NPAIRS * SLOTS), degree.reshape(NPAIRS * SLOTS), diffusivity)
    return solved * alive.reshape(NPAIRS * SLOTS)
```

```python
import functools

import jax
import jax.numpy as jnp
from jax import lax
from jax.experimental import pallas as pl
from jax.experimental.pallas import tpu as pltpu
from jax.sharding import PartitionSpec as P

LMAX = 511
ROTATION = 2.0
SHELL_RADIUS = 16.0
RADII = 8
VMEM_LIMIT = 56 * 1024 * 1024
MESH = pl.DeviceIdType.MESH


def slot_rows(lowest, slots):
    slot = lax.broadcasted_iota(jnp.int32, (1, slots), 1)
    first = slot < LMAX + 1 - lowest
    held = slot < LMAX + 2
    second = jnp.logical_and(jnp.logical_not(first), held)
    degree = jnp.where(first, lowest + slot, slot - 1)
    order = jnp.where(first, lowest, LMAX - lowest)
    return first, second, held, degree, order


def say_hello(barrier, axis_sizes):
    total = 0
    for axis, size in axis_sizes:
        me = lax.axis_index(axis)
        for k in range(1, size):
            pl.semaphore_signal(
                barrier, inc=1, device_id={axis: lax.rem(me + k, size)}, device_id_type=MESH
            )
        total += size - 1
    return total


def partner_table(n, pair, out):
    count = 2 * n
    rows = lax.broadcasted_iota(jnp.int32, (count, 128), 0)
    lanes = lax.broadcasted_iota(jnp.int32, (count, 128), 1)
    values = []
    for g in range(n):
        values += [pair[g], LMAX - pair[g]]
    to = jnp.zeros((count, 128), jnp.int32)
    of = jnp.zeros((count, 128), jnp.int32)
    for k, value in enumerate(values):
        to = jnp.where(rows == k, value, to)
        of = jnp.where(lanes == k, value, of)
    need = to - of
    size = jnp.abs(need)
    place = jnp.full((count, 128), 3 * count, jnp.int32)
    for k, value in enumerate(values):
        place = jnp.where(size == value, k, place)
    place = jnp.where(jnp.logical_and(need < 0, place < count), place + count, place)
    place = jnp.where(need == of, lanes + 2 * count, place)
    out[...] = jnp.where(need > of, 3 * count, place)


def step_kernel(
    n, rows_count, pair, diffusivity, spectra_hbm, dtheta_hbm, dphi_hbm, analysis_hbm,
    local_out, ends_out,
    spectra, dtheta, dphi, analysis, send, x, states, sums, got, edges, right, ahead, back,
    partner_rows, partner,
    load_sem, table_sem, send_sem, recv_sem, back_send, back_recv, edge_send, edge_recv,
):
    loads = [
        pltpu.make_async_copy(source, target, load_sem.at[i])
        for i, (source, target) in enumerate(
            [(spectra_hbm, spectra), (dtheta_hbm, dtheta), (dphi_hbm, dphi), (analysis_hbm, analysis)]
        )
    ]
    for load in loads:
        load.start()
    barrier = pltpu.get_barrier_semaphore()
    greetings = say_hello(barrier, [("ma", n), ("row", rows_count)])
    me = lax.axis_index("ma")
    row = lax.axis_index("row")
    slots = spectra.shape[3]
    points = spectra.shape[2]
    radii = RADII
    groups = points // radii
    halves = n // groups
    width = dtheta.shape[1] // halves
    chunks = width // 128
    orders = 2 * n

    partner_table(n, pair, partner_rows)
    table_copy = pltpu.make_async_copy(partner_rows, partner, table_sem.at[0])
    table_copy.start()

    keep = jnp.where(pair[me] == 0, 0.0, 1.0).astype(jnp.float32)
    lowest = pair[me]
    first, second, held, degree, order = slot_rows(lowest, slots)

    for load in loads[:3]:
        load.wait()

    def block_for(group, half):
        v = spectra[:, :, group * radii : (group + 1) * radii, :]
        v = v.reshape(8 * radii, slots)
        lhs = jnp.concatenate([jnp.where(first, v, 0.0), jnp.where(second, v, 0.0)], axis=0)
        lhs = lhs.astype(jnp.bfloat16)
        columns = slice(half * width, (half + 1) * width)
        t = jnp.dot(lhs, dtheta[:, columns], preferred_element_type=jnp.float32)
        d = jnp.dot(lhs, dphi[:, columns], preferred_element_type=jnp.float32)
        t = t.reshape(2, 4, 2, radii, width)
        d = d.reshape(2, 4, 2, radii, width)
        parts = []
        for j in range(2):
            z_t, w_t, s_t, a_t = (t[j, f] for f in range(4))
            z_d, w_d, s_d, a_d = (d[j, f] for f in range(4))
            pieces = [
                (w_t[0] + z_d[1], w_t[1] - z_d[0]),
                (z_t[0] - w_d[1], z_t[1] + w_d[0]),
                (s_t[0], s_t[1]),
                (-s_d[1], s_d[0]),
                (a_d[1], -a_d[0]),
                (a_t[0], a_t[1]),
            ]
            for real, imag in pieces:
                parts += [real, imag * keep if j == 0 else imag]
        return jnp.concatenate(parts, axis=0).astype(jnp.bfloat16)

    for group in range(groups):
        for half in range(halves):
            value = block_for(group, half)
            for c in range(chunks):
                send[c, group * halves + half] = value[:, c * 128 : (c + 1) * 128]

    def grid_copy(e, source, c):
        return pltpu.make_async_remote_copy(
            src_ref=send.at[c, e], dst_ref=x.at[c, source],
            send_sem=send_sem.at[c, e], recv_sem=recv_sem.at[c, source],
            device_id={"ma": e}, device_id_type=MESH,
        )

    def back_copy(e, source, c):
        return pltpu.make_async_remote_copy(
            src_ref=sums.at[c, e], dst_ref=got.at[c, source],
            send_sem=back_send.at[c, e], recv_sem=back_recv.at[c, source],
            device_id={"ma": e}, device_id_type=MESH,
        )

    tall = n // 4
    my_y, my_x, my_core = me // 4, lax.rem(me // 2, 2), lax.rem(me, 2)

    def target(k):
        dy, dx, dc = k // 4, (k // 2) % 2, k % 2
        return (
            lax.rem(my_y + dy, tall) * 4 + lax.rem(my_x + dx, 2) * 2 + lax.rem(my_core + dc, 2)
        )

    pl.semaphore_wait(barrier, greetings)
    for c in range(chunks):
        for k in range(n - 1, 0, -1):
            grid_copy(target(k), me, c).start()
    for c in range(chunks):
        x[c, me] = send[c, me]

    alive = held.astype(jnp.float32)
    l = degree.astype(jnp.float32)
    m = order.astype(jnp.float32)
    lower = jnp.sqrt((l * l - m * m) * alive / jnp.maximum(4.0 * l * l - 1.0, 1.0)) * ROTATION
    u = l + 1.0
    upper = jnp.sqrt(jnp.maximum((u * u - m * m) / (4.0 * u * u - 1.0), 0.0))
    upper = jnp.where(degree < LMAX, upper * alive, 0.0) * ROTATION
    spin = ROTATION * m / (l * (l + 1.0) + 2.0) * alive

    all_points = points * rows_count
    field = lax.broadcasted_iota(jnp.int32, (8, 1), 0) // 2
    nu = jnp.zeros((8, 1), jnp.float32)
    for f in range(4):
        nu = jnp.where(field == f, diffusivity[f], nu)
    off = nu * float((all_points + 1) ** 2)
    half_excess = (1.0 + nu * (l * (l + 1.0) / SHELL_RADIUS**2)) / (2.0 * off)
    root = jnp.sqrt(half_excess * half_excess + 2.0 * half_excess)
    inverse = 1.0 + half_excess + root
    rho = 1.0 / inverse
    log_rho = -jnp.log(inverse)
    inner = 1.0 / (2.0 * off * root)

    def power(exponent):
        return jnp.exp(log_rho * exponent)

    def couple(v):
        edge = jnp.zeros((points, 1), jnp.float32)
        below = jnp.concatenate([edge, v[:, : slots - 1]], axis=1)
        above = jnp.concatenate([v[:, 1:], edge], axis=1)
        return (lower * below + upper * above) * alive

    z0, z1 = (jnp.where(held, spectra[0, c], 0.0) for c in range(2))
    w0, w1 = (jnp.where(held, spectra[1, c], 0.0) for c in range(2))
    linear = [
        z0 - spin * z1 + couple(w0),
        z1 + spin * z0 + couple(w1),
        w0 - spin * w1 - couple(z0),
        w1 + spin * w0 - couple(z1),
    ]
    for f in (2, 3):
        for c in range(2):
            linear.append(jnp.where(held, spectra[f, c], 0.0))
    for g in range(groups):
        block = jnp.stack([v[g * radii : (g + 1) * radii] for v in linear], axis=0)
        right[g * radii : (g + 1) * radii] = jnp.swapaxes(block, 0, 1)

    before = (row * points).astype(jnp.float32)
    after = ((rows_count - 1 - row) * points).astype(jnp.float32)

    zero = jnp.zeros((radii, 128), jnp.float32)
    for q in range(12):
        states[3 * orders, q] = zero
    table_copy.wait()

    def chunk_step(c, carry):
        def arrive(k, carry):
            e = lax.rem(me + k, n)
            grid_copy(e, e, c).wait_recv()
            return carry

        lax.fori_loop(1, n, arrive, 0)

        def unpack(g, carry):
            block = x[c, g].astype(jnp.float32).reshape(2, 6, 2, radii, 128)
            for j in range(2):
                at_order = 2 * g + j
                u_t, u_p, s_t, s_p, b_t, b_p = (block[j, q] for q in range(6))
                for q, (p, t) in enumerate(((b_p, b_t), (u_p, u_t), (s_p, s_t))):
                    plus = (p[0] - t[1], p[1] + t[0])
                    minus = (p[0] + t[1], p[1] - t[0])
                    parts = (plus[0], plus[1], minus[0], minus[1])
                    turned = (minus[0], -minus[1], plus[0], -plus[1])
                    for i in range(4):
                        states[at_order, 4 * q + i] = parts[i]
                        states[orders + at_order, 4 * q + i] = turned[i]
                        states[2 * orders + at_order, 4 * q + i] = 0.5 * parts[i]
            return carry

        lax.fori_loop(0, n, unpack, 0)

        def one_order(i, carry):
            e = target(n - 1 - i // 2)
            j = lax.rem(i, 2)
            t = 2 * e + j

            def add(a, total):
                b = partner[t, a]
                vp, vm, yp, ym, wp, wm = (
                    (states[a, 2 * q], states[a, 2 * q + 1], states[b, 2 * q], states[b, 2 * q + 1])
                    for q in range(6)
                )

                def square(v):
                    ar, ai, br, bi = v
                    return ar * br - ai * bi, ar * bi + ai * br

                def cross(v, w):
                    ar, ai, br, bi = v
                    cr, ci, dr, di = w
                    return (
                        (ar * dr - ai * di) + (cr * br - ci * bi),
                        (ar * di + ai * dr) + (cr * bi + ci * br),
                    )

                terms = []
                for v, y in ((vp, yp), (vm, ym)):
                    first_term, second_term = square(v), square(y)
                    terms += [first_term[0] - second_term[0], first_term[1] - second_term[1]]
                heat, other = cross(ym, wp), cross(yp, wm)
                terms += [heat[0] + other[0], heat[1] + other[1]]
                bent, other = cross(ym, vp), cross(yp, vm)
                terms += [bent[0] - other[0], bent[1] - other[1]]
                return tuple(v + w for v, w in zip(total, terms))

            pr, pi, mr, mi, hr, hi, er, ei = lax.fori_loop(0, orders, add, (zero,) * 8, unroll=8)
            rows = [pi - mi, mr - pr, pr + mr, pi + mi, -hr, -hi, ei, -er]
            block = jnp.swapaxes(jnp.stack(rows, axis=0), 0, 1).reshape(8 * radii, 128)
            block = (0.5 * block).astype(jnp.bfloat16)
            sums[c, e, pl.ds(pl.multiple_of(j * 8 * radii, 8 * radii), 8 * radii), :] = block

            @pl.when(jnp.logical_and(j == 1, i < orders - 2))
            def _():
                back_copy(e, me, c).start()

            return carry

        lax.fori_loop(0, orders, one_order, 0)
        got[c, me] = sums[c, me]
        return carry

    lax.fori_loop(0, chunks, chunk_step, 0)
    loads[3].wait()

    contract = (((1,), (1,)), ((), ()))

    def project(c):
        for k in range(1, n):
            e = lax.rem(me + k, n)
            back_copy(e, e, c).wait_recv()
        rhs = jnp.concatenate(
            [analysis[:, h * width + c * 128 : h * width + (c + 1) * 128] for h in range(halves)], axis=1
        )
        for g in range(groups):
            lhs = jnp.concatenate([got[c, g * halves + h] for h in range(halves)], axis=1)
            total = lax.dot_general(lhs, rhs, contract, preferred_element_type=jnp.float32)
            total = total.reshape(2, radii, 8, slots)
            rows = slice(g * radii, (g + 1) * radii)
            right[rows] += jnp.where(first, total[0], jnp.where(second, total[1], 0.0))

    for c in range(chunks):
        project(c)

    up = right[0]
    down = right[points - 1]
    ahead[0] = up
    back[points - 1] = down
    for k in range(1, points):
        up = right[k] + rho * up
        down = right[points - 1 - k] + rho * down
        ahead[k] = up
        back[points - 1 - k] = down
    edges[row] = jnp.concatenate([up, down], axis=0).astype(jnp.bfloat16)

    def edge_copy(e, source):
        return pltpu.make_async_remote_copy(
            src_ref=edges.at[row], dst_ref=edges.at[source],
            send_sem=edge_send.at[e], recv_sem=edge_recv.at[source],
            device_id={"row": e}, device_id_type=MESH,
        )

    for k in range(1, rows_count):
        edge_copy(lax.rem(row + k, rows_count), row).start()

    local_out[points - 1] = inner * ahead[points - 1]
    for k in range(points - 1):
        local_out[k] = inner * (ahead[k] + rho * back[k + 1])

    span = power(float(all_points + 1))
    scale = 1.0 / (1.0 - span * span)
    to_start, to_end = power(before), power(after)
    shifts = [power(float(k * points)) for k in range(rows_count)]
    zero = jnp.zeros((8, slots), jnp.float32)
    weights, reverses = [], []
    for e in range(rows_count):
        weight, reverse = zero, zero
        for k in range(rows_count - 1):
            weight = jnp.where(row - 1 - e == k, shifts[k], weight)
            reverse = jnp.where(e - row - 1 == k, shifts[k], reverse)
        weights.append(weight)
        reverses.append(reverse)
    ends_out[2] = rho

    for c in range(chunks):
        for k in range(1, n):
            e = lax.rem(me + k, n)
            grid_copy(e, e, c).wait_send()
            back_copy(e, e, c).wait_send()
    for k in range(1, rows_count):
        e = lax.rem(row + k, rows_count)
        edge_copy(e, e).wait()

    ahead_in, back_in, ahead_all, back_all = zero, zero, zero, zero
    for e in range(rows_count):
        both = edges[e].astype(jnp.float32)
        f_e, g_e = both[0:8], both[8:16]
        ahead_in += weights[e] * f_e
        back_in += reverses[e] * g_e
        ahead_all += shifts[rows_count - 1 - e] * f_e
        back_all += shifts[e] * g_e
    low = inner * rho * back_all
    high = inner * rho * ahead_all
    ends_out[0] = inner * ahead_in + (span * high - low) * scale * to_start
    ends_out[1] = inner * back_in + (span * low - high) * scale * to_end


def finish_kernel(inside, ends, out):
    points, slots = inside.shape[0], inside.shape[2]
    for start in range(0, slots, 128):
        at = slice(start, min(start + 128, slots))
        rho = ends[2, :, at]
        from_start, from_end = ends[0, :, at], ends[1, :, at]
        values = [inside[k, :, at] for k in range(points)]
        for k in range(points):
            from_start = from_start * rho
            values[k] = values[k] + from_start
        for k in reversed(range(points)):
            from_end = from_end * rho
            values[k] = values[k] + from_end
        for g in range(0, points, RADII):
            block = jnp.swapaxes(jnp.stack(values[g : g + RADII], axis=0), 0, 1)
            out[:, g : g + RADII, at] = block


def local(n, rows_count, spectra, dtheta, dphi, analysis, pair_index, diffusivity):
    points, slots = spectra.shape[2], spectra.shape[3]
    radii = RADII
    halves = n * radii // points
    width = -(-dtheta.shape[1] // (128 * halves)) * 128
    extra = width * halves - dtheta.shape[1]
    if extra:
        dtheta, dphi, analysis = (jnp.pad(v, ((0, 0), (0, extra))) for v in (dtheta, dphi, analysis))
    chunks = width // 128
    vmem = pl.BlockSpec(memory_space=pltpu.VMEM)
    smem = pl.BlockSpec(memory_space=pltpu.SMEM)
    hbm = pl.BlockSpec(memory_space=pltpu.HBM)
    shape = spectra.shape
    table = pltpu.VMEM(dtheta.shape, jnp.bfloat16)
    turned = pltpu.VMEM((points, 8, slots), jnp.float32)
    inside, ends = pl.pallas_call(
        functools.partial(step_kernel, n, rows_count),
        out_shape=(
            pltpu.VMEM((points, 8, slots), jnp.float32),
            pltpu.VMEM((3, 8, slots), jnp.float32),
        ),
        in_specs=[smem, smem, hbm, hbm, hbm, hbm],
        out_specs=(vmem, vmem),
        scratch_shapes=[
            pltpu.VMEM(shape, jnp.float32),
            table,
            table,
            table,
            pltpu.VMEM((chunks, n, 24 * radii, 128), jnp.bfloat16),
            pltpu.VMEM((chunks, n, 24 * radii, 128), jnp.bfloat16),
            pltpu.VMEM((6 * n + 1, 12, radii, 128), jnp.float32),
            pltpu.VMEM((chunks, n, 16 * radii, 128), jnp.bfloat16),
            pltpu.VMEM((chunks, n, 16 * radii, 128), jnp.bfloat16),
            pltpu.VMEM((rows_count, 16, slots), jnp.bfloat16),
            turned,
            turned,
            turned,
            pltpu.VMEM((2 * n, 128), jnp.int32),
            pltpu.SMEM((2 * n, 128), jnp.int32),
            pltpu.SemaphoreType.DMA((4,)),
            pltpu.SemaphoreType.DMA((1,)),
            pltpu.SemaphoreType.DMA((chunks, n)),
            pltpu.SemaphoreType.DMA((chunks, n)),
            pltpu.SemaphoreType.DMA((chunks, n)),
            pltpu.SemaphoreType.DMA((chunks, n)),
            pltpu.SemaphoreType.DMA((rows_count,)),
            pltpu.SemaphoreType.DMA((rows_count,)),
        ],
        compiler_params=pltpu.CompilerParams(
            collective_id=0, has_side_effects=True, vmem_limit_bytes=VMEM_LIMIT
        ),
        name="step",
    )(pair_index, diffusivity, spectra, dtheta, dphi, analysis)
    result = pl.pallas_call(
        finish_kernel,
        out_shape=jax.ShapeDtypeStruct((8, points, slots), jnp.float32),
        in_specs=[vmem, vmem],
        out_specs=vmem,
        compiler_params=pltpu.CompilerParams(vmem_limit_bytes=8 * 1024 * 1024),
        name="finish",
    )(inside, ends)
    return result.reshape(shape)


def solution(mesh):
    n, rows_count = mesh.shape["ma"], mesh.shape["row"]
    return jax.shard_map(
        functools.partial(local, n, rows_count),
        mesh=mesh,
        in_specs=(
            P(None, None, "row", "ma"),
            P("ma", None),
            P("ma", None),
            P("ma", None),
            P(),
            P(),
        ),
        out_specs=P(None, None, "row", "ma"),
        check_vma=False,
    )
```

```python
import functools

import jax
import jax.numpy as jnp
from jax import lax
from jax.experimental import pallas as pl
from jax.experimental.pallas import tpu as pltpu
from jax.sharding import PartitionSpec as P

LMAX = 511
ROTATION = 2.0
SHELL_RADIUS = 16.0
RADII = 8
VMEM_LIMIT = 56 * 1024 * 1024
MESH = pl.DeviceIdType.MESH


def slot_rows(lowest, slots):
    slot = lax.broadcasted_iota(jnp.int32, (1, slots), 1)
    first = slot < LMAX + 1 - lowest
    held = slot < LMAX + 2
    second = jnp.logical_and(jnp.logical_not(first), held)
    degree = jnp.where(first, lowest + slot, slot - 1)
    order = jnp.where(first, lowest, LMAX - lowest)
    return first, second, held, degree, order


def say_hello(barrier, axis_sizes):
    total = 0
    for axis, size in axis_sizes:
        me = lax.axis_index(axis)
        for k in range(1, size):
            pl.semaphore_signal(
                barrier, inc=1, device_id={axis: lax.rem(me + k, size)}, device_id_type=MESH
            )
        total += size - 1
    return total


def partner_table(n, pair, out):
    count = 2 * n
    rows = lax.broadcasted_iota(jnp.int32, (count, 128), 0)
    lanes = lax.broadcasted_iota(jnp.int32, (count, 128), 1)
    values = []
    for g in range(n):
        values += [pair[g], LMAX - pair[g]]
    to = jnp.zeros((count, 128), jnp.int32)
    of = jnp.zeros((count, 128), jnp.int32)
    for k, value in enumerate(values):
        to = jnp.where(rows == k, value, to)
        of = jnp.where(lanes == k, value, of)
    need = to - of
    size = jnp.abs(need)
    place = jnp.full((count, 128), 3 * count, jnp.int32)
    for k, value in enumerate(values):
        place = jnp.where(size == value, k, place)
    place = jnp.where(jnp.logical_and(need < 0, place < count), place + count, place)
    place = jnp.where(need == of, lanes + 2 * count, place)
    out[...] = jnp.where(need > of, 3 * count, place)


def step_kernel(
    n, rows_count, pair_hbm, diffusivity_hbm, spectra_hbm, dtheta_hbm, dphi_hbm, analysis_hbm,
    local_out, ends_out, rise, fall,
    spectra, dtheta, dphi, analysis, send, x, states, sums, got, edges, right, ahead, back,
    partner_rows, partner, pair, diffusivity,
    load_sem, table_sem, send_sem, recv_sem, back_send, back_recv, edge_send, edge_recv,
):
    loads = [
        pltpu.make_async_copy(source, target, load_sem.at[i])
        for i, (source, target) in enumerate(
            [
                (pair_hbm, pair), (spectra_hbm, spectra), (dtheta_hbm, dtheta), (dphi_hbm, dphi),
                (diffusivity_hbm, diffusivity), (analysis_hbm, analysis),
            ]
        )
    ]
    barrier = pltpu.get_barrier_semaphore()
    greetings = say_hello(barrier, [("ma", n), ("row", rows_count)])
    for load in loads:
        load.start()
    me = lax.axis_index("ma")
    row = lax.axis_index("row")
    slots = spectra.shape[3]
    points = spectra.shape[2]
    radii = RADII
    groups = points // radii
    halves = n // groups
    width = dtheta.shape[1] // halves
    chunks = width // 128
    orders = 2 * n

    loads[0].wait()
    partner_table(n, pair, partner_rows)
    table_copy = pltpu.make_async_copy(partner_rows, partner, table_sem.at[0])
    table_copy.start()

    keep = jnp.where(pair[me] == 0, 0.0, 1.0).astype(jnp.float32)
    lowest = pair[me]
    first, second, held, degree, order = slot_rows(lowest, slots)

    loads[1].wait()
    lhs = []
    for g in range(groups):
        v = spectra[:, :, g * radii : (g + 1) * radii, :].reshape(8 * radii, slots)
        lhs += [jnp.where(first, v, 0.0), jnp.where(second, v, 0.0)]
    lhs = jnp.concatenate(lhs, axis=0).astype(jnp.bfloat16)

    def grid_block(t, d):
        parts = []
        for j in range(2):
            z_t, w_t, s_t, a_t = (t[j, f] for f in range(4))
            z_d, w_d, s_d, a_d = (d[j, f] for f in range(4))
            pieces = [
                (w_t[0] + z_d[1], w_t[1] - z_d[0]),
                (z_t[0] - w_d[1], z_t[1] + w_d[0]),
                (s_t[0], s_t[1]),
                (-s_d[1], s_d[0]),
                (a_d[1], -a_d[0]),
                (a_t[0], a_t[1]),
            ]
            for real, imag in pieces:
                parts += [real, imag * keep if j == 0 else imag]
        return jnp.concatenate(parts, axis=0).astype(jnp.bfloat16)

    loads[2].wait()
    loads[3].wait()
    block = 256 if (width * halves) % 256 == 0 else 128
    for start in range(0, width * halves, block):
        t, d = (
            jnp.dot(lhs, v[:, start : start + block], preferred_element_type=jnp.float32)
            for v in (dtheta, dphi)
        )
        t = t.reshape(groups, 2, 4, 2, radii, block)
        d = d.reshape(groups, 2, 4, 2, radii, block)
        for at in range(start, start + block, 128):
            half, c = at // width, at % width // 128
            here = slice(at - start, at - start + 128)
            for g in range(groups):
                send[c, g * halves + half] = grid_block(t[g, ..., here], d[g, ..., here])

    def grid_copy(e, source, c):
        return pltpu.make_async_remote_copy(
            src_ref=send.at[c, e], dst_ref=x.at[c, source],
            send_sem=send_sem.at[c, e], recv_sem=recv_sem.at[c, source],
            device_id={"ma": e}, device_id_type=MESH,
        )

    def back_copy(e, source, c):
        return pltpu.make_async_remote_copy(
            src_ref=sums.at[c, e], dst_ref=got.at[c, source],
            send_sem=back_send.at[c, e], recv_sem=back_recv.at[c, source],
            device_id={"ma": e}, device_id_type=MESH,
        )

    tall = n // 4
    my_y, my_x, my_core = me // 4, lax.rem(me // 2, 2), lax.rem(me, 2)

    def target(k):
        dy, dx, dc = k // 4, (k // 2) % 2, k % 2
        return (
            lax.rem(my_y + dy, tall) * 4 + lax.rem(my_x + dx, 2) * 2 + lax.rem(my_core + dc, 2)
        )

    pl.semaphore_wait(barrier, greetings)
    for c in range(chunks):
        for k in range(n - 1, 0, -1):
            grid_copy(target(k), me, c).start()
    for c in range(chunks):
        x[c, me] = send[c, me]

    alive = held.astype(jnp.float32)
    l = degree.astype(jnp.float32)
    m = order.astype(jnp.float32)
    lower = jnp.sqrt((l * l - m * m) * alive / jnp.maximum(4.0 * l * l - 1.0, 1.0)) * ROTATION
    u = l + 1.0
    upper = jnp.sqrt(jnp.maximum((u * u - m * m) / (4.0 * u * u - 1.0), 0.0))
    upper = jnp.where(degree < LMAX, upper * alive, 0.0) * ROTATION
    spin = ROTATION * m / (l * (l + 1.0) + 2.0) * alive

    loads[4].wait()
    all_points = points * rows_count
    field = lax.broadcasted_iota(jnp.int32, (8, 1), 0) // 2
    nu = jnp.zeros((8, 1), jnp.float32)
    for f in range(4):
        nu = jnp.where(field == f, diffusivity[f], nu)
    off = nu * float((all_points + 1) ** 2)
    half_excess = (1.0 + nu * (l * (l + 1.0) / SHELL_RADIUS**2)) / (2.0 * off)
    root = jnp.sqrt(half_excess * half_excess + 2.0 * half_excess)
    inverse = 1.0 + half_excess + root
    rho = 1.0 / inverse
    log_rho = -jnp.log(inverse)
    inner = 1.0 / (2.0 * off * root)

    def power(exponent):
        return jnp.exp(log_rho * exponent)

    def couple(v):
        edge = jnp.zeros((points, 1), jnp.float32)
        below = jnp.concatenate([edge, v[:, : slots - 1]], axis=1)
        above = jnp.concatenate([v[:, 1:], edge], axis=1)
        return (lower * below + upper * above) * alive

    z0, z1 = (jnp.where(held, spectra[0, c], 0.0) for c in range(2))
    w0, w1 = (jnp.where(held, spectra[1, c], 0.0) for c in range(2))
    linear = [
        z0 - spin * z1 + couple(w0),
        z1 + spin * z0 + couple(w1),
        w0 - spin * w1 - couple(z0),
        w1 + spin * w0 - couple(z1),
    ]
    for f in (2, 3):
        for c in range(2):
            linear.append(jnp.where(held, spectra[f, c], 0.0))
    for g in range(groups):
        block = jnp.stack([v[g * radii : (g + 1) * radii] for v in linear], axis=0)
        right[g * radii : (g + 1) * radii] = jnp.swapaxes(block, 0, 1)

    at = lax.broadcasted_iota(jnp.int32, (points, slots), 0)
    for f in range(4):
        log_here = log_rho[2 * f : 2 * f + 1]
        rise[f] = jnp.exp(log_here * (at + 1).astype(jnp.float32))
        fall[f] = jnp.exp(log_here * (points - at).astype(jnp.float32))

    before = (row * points).astype(jnp.float32)
    after = ((rows_count - 1 - row) * points).astype(jnp.float32)

    zero = jnp.zeros((radii, 128), jnp.float32)
    for q in range(12):
        states[3 * orders, q] = zero
    table_copy.wait()

    def chunk_step(c, carry):
        def unpack(k, carry):
            g = target(k)

            @pl.when(k > 0)
            def _():
                grid_copy(g, g, c).wait_recv()

            block = x[c, g].astype(jnp.float32).reshape(2, 6, 2, radii, 128)
            for j in range(2):
                at_order = 2 * g + j
                u_t, u_p, s_t, s_p, b_t, b_p = (block[j, q] for q in range(6))
                for q, (p, t) in enumerate(((b_p, b_t), (u_p, u_t), (s_p, s_t))):
                    plus = (p[0] - t[1], p[1] + t[0])
                    minus = (p[0] + t[1], p[1] - t[0])
                    parts = (plus[0], plus[1], minus[0], minus[1])
                    turned = (minus[0], -minus[1], plus[0], -plus[1])
                    for i in range(4):
                        states[at_order, 4 * q + i] = parts[i]
                        states[orders + at_order, 4 * q + i] = turned[i]
                        states[2 * orders + at_order, 4 * q + i] = 0.5 * parts[i]
            return carry

        lax.fori_loop(0, n, unpack, 0)

        def one_order(i, carry):
            e = target(n - 1 - i // 2)
            j = lax.rem(i, 2)
            t = 2 * e + j

            def add(a, total):
                b = partner[t, a]
                vp, vm, yp, ym, wp, wm = (
                    (states[a, 2 * q], states[a, 2 * q + 1], states[b, 2 * q], states[b, 2 * q + 1])
                    for q in range(6)
                )

                def square(v):
                    ar, ai, br, bi = v
                    return ar * br - ai * bi, ar * bi + ai * br

                def cross(v, w):
                    ar, ai, br, bi = v
                    cr, ci, dr, di = w
                    return (
                        (ar * dr - ai * di) + (cr * br - ci * bi),
                        (ar * di + ai * dr) + (cr * bi + ci * br),
                    )

                terms = []
                for v, y in ((vp, yp), (vm, ym)):
                    first_term, second_term = square(v), square(y)
                    terms += [first_term[0] - second_term[0], first_term[1] - second_term[1]]
                heat, other = cross(ym, wp), cross(yp, wm)
                terms += [heat[0] + other[0], heat[1] + other[1]]
                bent, other = cross(ym, vp), cross(yp, vm)
                terms += [bent[0] - other[0], bent[1] - other[1]]
                return tuple(v + w for v, w in zip(total, terms))

            pr, pi, mr, mi, hr, hi, er, ei = lax.fori_loop(0, orders, add, (zero,) * 8, unroll=8)
            rows = [pi - mi, mr - pr, pr + mr, pi + mi, -hr, -hi, ei, -er]
            block = jnp.swapaxes(jnp.stack(rows, axis=0), 0, 1).reshape(8 * radii, 128)
            block = (0.5 * block).astype(jnp.bfloat16)
            sums[c, e, pl.ds(pl.multiple_of(j * 8 * radii, 8 * radii), 8 * radii), :] = block

            @pl.when(jnp.logical_and(j == 1, i < orders - 2))
            def _():
                back_copy(e, me, c).start()

            return carry

        lax.fori_loop(0, orders, one_order, 0)
        got[c, me] = sums[c, me]
        return carry

    lax.fori_loop(0, chunks, chunk_step, 0)
    loads[5].wait()

    contract = (((1,), (1,)), ((), ()))

    def project(c):
        for k in range(1, n):
            e = lax.rem(me + k, n)
            back_copy(e, e, c).wait_recv()
        rhs = jnp.concatenate(
            [analysis[:, h * width + c * 128 : h * width + (c + 1) * 128] for h in range(halves)], axis=1
        )
        for g in range(groups):
            lhs = jnp.concatenate([got[c, g * halves + h] for h in range(halves)], axis=1)
            total = lax.dot_general(lhs, rhs, contract, preferred_element_type=jnp.float32)
            total = total.reshape(2, radii, 8, slots)
            rows = slice(g * radii, (g + 1) * radii)
            right[rows] += jnp.where(first, total[0], jnp.where(second, total[1], 0.0))

    for c in range(chunks):
        project(c)

    up = right[0]
    down = right[points - 1]
    ahead[0] = up
    back[points - 1] = down
    for k in range(1, points):
        up = right[k] + rho * up
        down = right[points - 1 - k] + rho * down
        ahead[k] = up
        back[points - 1 - k] = down
    edges[row] = jnp.concatenate([up, down], axis=0).astype(jnp.bfloat16)

    def edge_copy(e, source):
        return pltpu.make_async_remote_copy(
            src_ref=edges.at[row], dst_ref=edges.at[source],
            send_sem=edge_send.at[e], recv_sem=edge_recv.at[source],
            device_id={"row": e}, device_id_type=MESH,
        )

    for k in range(1, rows_count):
        edge_copy(lax.rem(row + k, rows_count), row).start()

    for g in range(groups):
        values = []
        for k in range(g * radii, (g + 1) * radii):
            value = ahead[k] + rho * back[k + 1] if k < points - 1 else ahead[k]
            values.append(inner * value)
        local_out[:, g * radii : (g + 1) * radii] = jnp.swapaxes(jnp.stack(values, axis=0), 0, 1)

    span = power(float(all_points + 1))
    scale = 1.0 / (1.0 - span * span)
    to_start, to_end = power(before), power(after)
    shifts = [power(float(k * points)) for k in range(rows_count)]
    zero = jnp.zeros((8, slots), jnp.float32)
    weights, reverses = [], []
    for e in range(rows_count):
        weight, reverse = zero, zero
        for k in range(rows_count - 1):
            weight = jnp.where(row - 1 - e == k, shifts[k], weight)
            reverse = jnp.where(e - row - 1 == k, shifts[k], reverse)
        weights.append(weight)
        reverses.append(reverse)

    for c in range(chunks):
        for k in range(1, n):
            e = lax.rem(me + k, n)
            grid_copy(e, e, c).wait_send()
            back_copy(e, e, c).wait_send()
    for k in range(1, rows_count):
        e = lax.rem(row + k, rows_count)
        edge_copy(e, e).wait()

    ahead_in, back_in, ahead_all, back_all = zero, zero, zero, zero
    for e in range(rows_count):
        both = edges[e].astype(jnp.float32)
        f_e, g_e = both[0:8], both[8:16]
        ahead_in += weights[e] * f_e
        back_in += reverses[e] * g_e
        ahead_all += shifts[rows_count - 1 - e] * f_e
        back_all += shifts[e] * g_e
    low = inner * rho * back_all
    high = inner * rho * ahead_all
    ends_out[0] = inner * ahead_in + (span * high - low) * scale * to_start
    ends_out[1] = inner * back_in + (span * low - high) * scale * to_end


def finish_kernel(inside, ends, rise, fall, out, result, sem):
    copies = []
    for q in range(8):
        left, right = ends[0, q : q + 1], ends[1, q : q + 1]
        result[q] = inside[q] + left * rise[q // 2] + right * fall[q // 2]
        copies.append(pltpu.make_async_copy(result.at[q], out.at[q], sem.at[q]))
        copies[-1].start()
    for copy in copies:
        copy.wait()


def local(n, rows_count, spectra, dtheta, dphi, analysis, pair_index, diffusivity):
    points, slots = spectra.shape[2], spectra.shape[3]
    radii = RADII
    halves = n * radii // points
    width = -(-dtheta.shape[1] // (128 * halves)) * 128
    extra = width * halves - dtheta.shape[1]
    if extra:
        dtheta, dphi, analysis = (jnp.pad(v, ((0, 0), (0, extra))) for v in (dtheta, dphi, analysis))
    chunks = width // 128
    vmem = pl.BlockSpec(memory_space=pltpu.VMEM)
    hbm = pl.BlockSpec(memory_space=pltpu.HBM)
    shape = spectra.shape
    table = pltpu.VMEM(dtheta.shape, jnp.bfloat16)
    turned = pltpu.VMEM((points, 8, slots), jnp.float32)
    inside, ends, rise, fall = pl.pallas_call(
        functools.partial(step_kernel, n, rows_count),
        out_shape=(
            pltpu.VMEM((8, points, slots), jnp.float32),
            pltpu.VMEM((2, 8, slots), jnp.float32),
            pltpu.VMEM((4, points, slots), jnp.float32),
            pltpu.VMEM((4, points, slots), jnp.float32),
        ),
        in_specs=[hbm] * 6,
        out_specs=(vmem,) * 4,
        scratch_shapes=[
            pltpu.VMEM(shape, jnp.float32),
            table,
            table,
            table,
            pltpu.VMEM((chunks, n, 24 * radii, 128), jnp.bfloat16),
            pltpu.VMEM((chunks, n, 24 * radii, 128), jnp.bfloat16),
            pltpu.VMEM((6 * n + 1, 12, radii, 128), jnp.float32),
            pltpu.VMEM((chunks, n, 16 * radii, 128), jnp.bfloat16),
            pltpu.VMEM((chunks, n, 16 * radii, 128), jnp.bfloat16),
            pltpu.VMEM((rows_count, 16, slots), jnp.bfloat16),
            turned,
            turned,
            turned,
            pltpu.VMEM((2 * n, 128), jnp.int32),
            pltpu.SMEM((2 * n, 128), jnp.int32),
            pltpu.SMEM(pair_index.shape, jnp.int32),
            pltpu.SMEM(diffusivity.shape, jnp.float32),
            pltpu.SemaphoreType.DMA((6,)),
            pltpu.SemaphoreType.DMA((1,)),
            pltpu.SemaphoreType.DMA((chunks, n)),
            pltpu.SemaphoreType.DMA((chunks, n)),
            pltpu.SemaphoreType.DMA((chunks, n)),
            pltpu.SemaphoreType.DMA((chunks, n)),
            pltpu.SemaphoreType.DMA((rows_count,)),
            pltpu.SemaphoreType.DMA((rows_count,)),
        ],
        compiler_params=pltpu.CompilerParams(
            collective_id=0, has_side_effects=True, vmem_limit_bytes=VMEM_LIMIT
        ),
        name="step",
    )(pair_index, diffusivity, spectra, dtheta, dphi, analysis)
    result = pl.pallas_call(
        finish_kernel,
        out_shape=jax.ShapeDtypeStruct((8, points, slots), jnp.float32),
        in_specs=[vmem] * 4,
        out_specs=hbm,
        scratch_shapes=[
            pltpu.VMEM((8, points, slots), jnp.float32), pltpu.SemaphoreType.DMA((8,))
        ],
        compiler_params=pltpu.CompilerParams(vmem_limit_bytes=8 * 1024 * 1024),
        name="finish",
    )(inside, ends, rise, fall)
    return result.reshape(shape)


def solution(mesh):
    n, rows_count = mesh.shape["ma"], mesh.shape["row"]
    return jax.shard_map(
        functools.partial(local, n, rows_count),
        mesh=mesh,
        in_specs=(
            P(None, None, "row", "ma"),
            P("ma", None),
            P("ma", None),
            P("ma", None),
            P(),
            P(),
        ),
        out_specs=P(None, None, "row", "ma"),
        check_vma=False,
    )
```

```python
import functools

import jax
import jax.numpy as jnp
from jax import lax
from jax.experimental import pallas as pl
from jax.experimental.pallas import tpu as pltpu
from jax.sharding import PartitionSpec as P

LMAX = 511
ROTATION = 2.0
SHELL_RADIUS = 16.0
RADII = 8
VMEM_LIMIT = 56 * 1024 * 1024
MESH = pl.DeviceIdType.MESH


def slot_rows(lowest, slots):
    slot = lax.broadcasted_iota(jnp.int32, (1, slots), 1)
    first = slot < LMAX + 1 - lowest
    held = slot < LMAX + 2
    second = jnp.logical_and(jnp.logical_not(first), held)
    degree = jnp.where(first, lowest + slot, slot - 1)
    order = jnp.where(first, lowest, LMAX - lowest)
    return first, second, held, degree, order


def say_hello(barrier, axis_sizes):
    total = 0
    for axis, size in axis_sizes:
        me = lax.axis_index(axis)
        for k in range(1, size):
            pl.semaphore_signal(
                barrier, inc=1, device_id={axis: lax.rem(me + k, size)}, device_id_type=MESH
            )
        total += size - 1
    return total


def partner_table(n, pair, out):
    count = 2 * n
    rows = lax.broadcasted_iota(jnp.int32, (count, 128), 0)
    lanes = lax.broadcasted_iota(jnp.int32, (count, 128), 1)
    values = []
    for g in range(n):
        values += [pair[g], LMAX - pair[g]]
    to = jnp.zeros((count, 128), jnp.int32)
    of = jnp.zeros((count, 128), jnp.int32)
    for k, value in enumerate(values):
        to = jnp.where(rows == k, value, to)
        of = jnp.where(lanes == k, value, of)
    need = to - of
    size = jnp.abs(need)
    place = jnp.full((count, 128), 3 * count, jnp.int32)
    for k, value in enumerate(values):
        place = jnp.where(size == value, k, place)
    place = jnp.where(jnp.logical_and(need < 0, place < count), place + count, place)
    place = jnp.where(need == of, lanes + 2 * count, place)
    out[...] = jnp.where(need > of, 3 * count, place)


def step_kernel(
    n, rows_count, pair_hbm, diffusivity_hbm, spectra_hbm, dtheta_hbm, dphi_hbm, analysis_hbm,
    local_out, ends_out, rise, fall,
    spectra, dtheta, dphi, analysis, send, x, states, sums, got, edges, right, ahead, back,
    partner_rows, partner, pair, diffusivity,
    load_sem, piece_sem, table_sem, send_sem, recv_sem, back_send, back_recv, edge_send, edge_recv,
):
    me = lax.axis_index("ma")
    row = lax.axis_index("row")
    slots = spectra.shape[3]
    points = spectra.shape[2]
    radii = RADII
    groups = points // radii
    halves = n // groups
    chunks = dtheta.shape[0]
    width = chunks * 128
    orders = 2 * n

    def piece(i, c, h):
        source, place = ((dtheta_hbm, dtheta), (dphi_hbm, dphi), (analysis_hbm, analysis))[i]
        columns = slice(h * width + c * 128, h * width + (c + 1) * 128)
        return pltpu.make_async_copy(
            source.at[:, columns], place.at[c, :, h * 128 : (h + 1) * 128], piece_sem.at[i, c, h]
        )

    loads = [
        pltpu.make_async_copy(source, place, load_sem.at[i])
        for i, (source, place) in enumerate(
            [(pair_hbm, pair), (spectra_hbm, spectra), (diffusivity_hbm, diffusivity)]
        )
    ]
    barrier = pltpu.get_barrier_semaphore()
    greetings = say_hello(barrier, [("ma", n), ("row", rows_count)])
    loads[0].start()
    loads[1].start()
    for c in range(chunks):
        for h in range(halves):
            piece(0, c, h).start()
            piece(1, c, h).start()
    loads[2].start()
    for c in range(chunks):
        for h in range(halves):
            piece(2, c, h).start()

    loads[0].wait()
    partner_table(n, pair, partner_rows)
    table_copy = pltpu.make_async_copy(partner_rows, partner, table_sem.at[0])
    table_copy.start()

    keep = jnp.where(pair[me] == 0, 0.0, 1.0).astype(jnp.float32)
    lowest = pair[me]
    first, second, held, degree, order = slot_rows(lowest, slots)

    loads[1].wait()
    lhs = []
    for g in range(groups):
        v = spectra[:, :, g * radii : (g + 1) * radii, :].reshape(8 * radii, slots)
        lhs += [jnp.where(first, v, 0.0), jnp.where(second, v, 0.0)]
    lhs = jnp.concatenate(lhs, axis=0).astype(jnp.bfloat16)

    def grid_block(t, d):
        parts = []
        for j in range(2):
            z_t, w_t, s_t, a_t = (t[j, f] for f in range(4))
            z_d, w_d, s_d, a_d = (d[j, f] for f in range(4))
            pieces = [
                (w_t[0] + z_d[1], w_t[1] - z_d[0]),
                (z_t[0] - w_d[1], z_t[1] + w_d[0]),
                (s_t[0], s_t[1]),
                (-s_d[1], s_d[0]),
                (a_d[1], -a_d[0]),
                (a_t[0], a_t[1]),
            ]
            for real, imag in pieces:
                parts += [real, imag * keep if j == 0 else imag]
        return jnp.concatenate(parts, axis=0).astype(jnp.bfloat16)

    def grid_copy(e, source, c):
        return pltpu.make_async_remote_copy(
            src_ref=send.at[c, e], dst_ref=x.at[c, source],
            send_sem=send_sem.at[c, e], recv_sem=recv_sem.at[c, source],
            device_id={"ma": e}, device_id_type=MESH,
        )

    def back_copy(e, source, c):
        return pltpu.make_async_remote_copy(
            src_ref=sums.at[c, e], dst_ref=got.at[c, source],
            send_sem=back_send.at[c, e], recv_sem=back_recv.at[c, source],
            device_id={"ma": e}, device_id_type=MESH,
        )

    tall = n // 4
    my_y, my_x, my_core = me // 4, lax.rem(me // 2, 2), lax.rem(me, 2)

    def target(k):
        dy, dx, dc = k // 4, (k // 2) % 2, k % 2
        return (
            lax.rem(my_y + dy, tall) * 4 + lax.rem(my_x + dx, 2) * 2 + lax.rem(my_core + dc, 2)
        )

    for c in range(chunks):
        for h in range(halves):
            piece(0, c, h).wait()
            piece(1, c, h).wait()
        t, d = (jnp.dot(lhs, v[c], preferred_element_type=jnp.float32) for v in (dtheta, dphi))
        t = t.reshape(groups, 2, 4, 2, radii, halves * 128)
        d = d.reshape(groups, 2, 4, 2, radii, halves * 128)
        for g in range(groups):
            for h in range(halves):
                here = slice(h * 128, (h + 1) * 128)
                send[c, g * halves + h] = grid_block(t[g, ..., here], d[g, ..., here])
        if c == 0:
            pl.semaphore_wait(barrier, greetings)
        for k in range(n - 1, 0, -1):
            grid_copy(target(k), me, c).start()
        x[c, me] = send[c, me]

    near_first = sorted(range(n), key=lambda e: (e // 4 + e // 2 % 2 + e % 2, -e))

    def served(k):
        e = near_first[0]
        for at in range(1, n):
            e = jnp.where(k == at, near_first[at], e)
        return e

    alive = held.astype(jnp.float32)
    l = degree.astype(jnp.float32)
    m = order.astype(jnp.float32)
    lower = jnp.sqrt((l * l - m * m) * alive / jnp.maximum(4.0 * l * l - 1.0, 1.0)) * ROTATION
    u = l + 1.0
    upper = jnp.sqrt(jnp.maximum((u * u - m * m) / (4.0 * u * u - 1.0), 0.0))
    upper = jnp.where(degree < LMAX, upper * alive, 0.0) * ROTATION
    spin = ROTATION * m / (l * (l + 1.0) + 2.0) * alive

    loads[2].wait()
    all_points = points * rows_count
    field = lax.broadcasted_iota(jnp.int32, (8, 1), 0) // 2
    nu = jnp.zeros((8, 1), jnp.float32)
    for f in range(4):
        nu = jnp.where(field == f, diffusivity[f], nu)
    off = nu * float((all_points + 1) ** 2)
    half_excess = (1.0 + nu * (l * (l + 1.0) / SHELL_RADIUS**2)) / (2.0 * off)
    root = jnp.sqrt(half_excess * half_excess + 2.0 * half_excess)
    inverse = 1.0 + half_excess + root
    rho = 1.0 / inverse
    log_rho = -jnp.log(inverse)
    inner = 1.0 / (2.0 * off * root)

    def power(exponent):
        return jnp.exp(log_rho * exponent)

    def couple(v):
        edge = jnp.zeros((points, 1), jnp.float32)
        below = jnp.concatenate([edge, v[:, : slots - 1]], axis=1)
        above = jnp.concatenate([v[:, 1:], edge], axis=1)
        return (lower * below + upper * above) * alive

    z0, z1 = (jnp.where(held, spectra[0, c], 0.0) for c in range(2))
    w0, w1 = (jnp.where(held, spectra[1, c], 0.0) for c in range(2))
    linear = [
        z0 - spin * z1 + couple(w0),
        z1 + spin * z0 + couple(w1),
        w0 - spin * w1 - couple(z0),
        w1 + spin * w0 - couple(z1),
    ]
    for f in (2, 3):
        for c in range(2):
            linear.append(jnp.where(held, spectra[f, c], 0.0))
    for g in range(groups):
        block = jnp.stack([v[g * radii : (g + 1) * radii] for v in linear], axis=0)
        right[g * radii : (g + 1) * radii] = jnp.swapaxes(block, 0, 1)

    at = lax.broadcasted_iota(jnp.int32, (points, slots), 0)
    for f in range(4):
        log_here = log_rho[2 * f : 2 * f + 1]
        rise[f] = jnp.exp(log_here * (at + 1).astype(jnp.float32))
        fall[f] = jnp.exp(log_here * (points - at).astype(jnp.float32))

    before = (row * points).astype(jnp.float32)
    after = ((rows_count - 1 - row) * points).astype(jnp.float32)

    zero = jnp.zeros((radii, 128), jnp.float32)
    for q in range(12):
        states[3 * orders, q] = zero
    table_copy.wait()

    def chunk_step(c, carry):
        def unpack(k, carry):
            g = target(k)

            @pl.when(k > 0)
            def _():
                grid_copy(g, g, c).wait_recv()

            block = x[c, g].astype(jnp.float32).reshape(2, 6, 2, radii, 128)
            for j in range(2):
                at_order = 2 * g + j
                u_t, u_p, s_t, s_p, b_t, b_p = (block[j, q] for q in range(6))
                for q, (p, t) in enumerate(((b_p, b_t), (u_p, u_t), (s_p, s_t))):
                    plus = (p[0] - t[1], p[1] + t[0])
                    minus = (p[0] + t[1], p[1] - t[0])
                    parts = (plus[0], plus[1], minus[0], minus[1])
                    turned = (minus[0], -minus[1], plus[0], -plus[1])
                    for i in range(4):
                        states[at_order, 4 * q + i] = parts[i]
                        states[orders + at_order, 4 * q + i] = turned[i]
                        states[2 * orders + at_order, 4 * q + i] = 0.5 * parts[i]
            return carry

        lax.fori_loop(0, n, unpack, 0)

        def one_order(i, carry):
            e = served(i // 2)
            j = lax.rem(i, 2)
            t = 2 * e + j

            def add(a, total):
                b = partner[t, a]
                vp, vm, yp, ym, wp, wm = (
                    (states[a, 2 * q], states[a, 2 * q + 1], states[b, 2 * q], states[b, 2 * q + 1])
                    for q in range(6)
                )

                def square(v):
                    ar, ai, br, bi = v
                    return ar * br - ai * bi, ar * bi + ai * br

                def cross(v, w):
                    ar, ai, br, bi = v
                    cr, ci, dr, di = w
                    return (
                        (ar * dr - ai * di) + (cr * br - ci * bi),
                        (ar * di + ai * dr) + (cr * bi + ci * br),
                    )

                terms = []
                for v, y in ((vp, yp), (vm, ym)):
                    first_term, second_term = square(v), square(y)
                    terms += [first_term[0] - second_term[0], first_term[1] - second_term[1]]
                heat, other = cross(ym, wp), cross(yp, wm)
                terms += [heat[0] + other[0], heat[1] + other[1]]
                bent, other = cross(ym, vp), cross(yp, vm)
                terms += [bent[0] - other[0], bent[1] - other[1]]
                return tuple(v + w for v, w in zip(total, terms))

            pr, pi, mr, mi, hr, hi, er, ei = lax.fori_loop(0, orders, add, (zero,) * 8, unroll=8)
            rows = [pi - mi, mr - pr, pr + mr, pi + mi, -hr, -hi, ei, -er]
            block = jnp.swapaxes(jnp.stack(rows, axis=0), 0, 1).reshape(8 * radii, 128)
            block = (0.5 * block).astype(jnp.bfloat16)
            sums[c, e, pl.ds(pl.multiple_of(j * 8 * radii, 8 * radii), 8 * radii), :] = block

            @pl.when(jnp.logical_and(j == 1, e != me))
            def _():
                back_copy(e, me, c).start()

            return carry

        lax.fori_loop(0, orders, one_order, 0)
        got[c, me] = sums[c, me]
        return carry

    lax.fori_loop(0, chunks, chunk_step, 0)
    for c in range(chunks):
        for h in range(halves):
            piece(2, c, h).wait()

    contract = (((1,), (1,)), ((), ()))

    def project(c):
        for k in range(1, n):
            e = lax.rem(me + k, n)
            back_copy(e, e, c).wait_recv()
        for g in range(groups):
            lhs = jnp.concatenate([got[c, g * halves + h] for h in range(halves)], axis=1)
            total = lax.dot_general(lhs, analysis[c], contract, preferred_element_type=jnp.float32)
            total = total.reshape(2, radii, 8, slots)
            rows = slice(g * radii, (g + 1) * radii)
            right[rows] += jnp.where(first, total[0], jnp.where(second, total[1], 0.0))

    for c in range(chunks):
        project(c)

    up = right[0]
    down = right[points - 1]
    ahead[0] = up
    back[points - 1] = down
    for k in range(1, points):
        up = right[k] + rho * up
        down = right[points - 1 - k] + rho * down
        ahead[k] = up
        back[points - 1 - k] = down
    edges[row] = jnp.concatenate([up, down], axis=0).astype(jnp.bfloat16)

    def edge_copy(e, source):
        return pltpu.make_async_remote_copy(
            src_ref=edges.at[row], dst_ref=edges.at[source],
            send_sem=edge_send.at[e], recv_sem=edge_recv.at[source],
            device_id={"row": e}, device_id_type=MESH,
        )

    for k in range(1, rows_count):
        edge_copy(lax.rem(row + k, rows_count), row).start()

    for g in range(groups):
        values = []
        for k in range(g * radii, (g + 1) * radii):
            value = ahead[k] + rho * back[k + 1] if k < points - 1 else ahead[k]
            values.append(inner * value)
        local_out[:, g * radii : (g + 1) * radii] = jnp.swapaxes(jnp.stack(values, axis=0), 0, 1)

    span = power(float(all_points + 1))
    scale = 1.0 / (1.0 - span * span)
    to_start, to_end = power(before), power(after)
    shifts = [power(float(k * points)) for k in range(rows_count)]
    zero = jnp.zeros((8, slots), jnp.float32)
    weights, reverses = [], []
    for e in range(rows_count):
        weight, reverse = zero, zero
        for k in range(rows_count - 1):
            weight = jnp.where(row - 1 - e == k, shifts[k], weight)
            reverse = jnp.where(e - row - 1 == k, shifts[k], reverse)
        weights.append(weight)
        reverses.append(reverse)

    for c in range(chunks):
        for k in range(1, n):
            e = lax.rem(me + k, n)
            grid_copy(e, e, c).wait_send()
            back_copy(e, e, c).wait_send()
    for k in range(1, rows_count):
        e = lax.rem(row + k, rows_count)
        edge_copy(e, e).wait()

    ahead_in, back_in, ahead_all, back_all = zero, zero, zero, zero
    for e in range(rows_count):
        both = edges[e].astype(jnp.float32)
        f_e, g_e = both[0:8], both[8:16]
        ahead_in += weights[e] * f_e
        back_in += reverses[e] * g_e
        ahead_all += shifts[rows_count - 1 - e] * f_e
        back_all += shifts[e] * g_e
    low = inner * rho * back_all
    high = inner * rho * ahead_all
    ends_out[0] = inner * ahead_in + (span * high - low) * scale * to_start
    ends_out[1] = inner * back_in + (span * low - high) * scale * to_end


def finish_kernel(inside, ends, rise, fall, out, result, sem):
    copies = []
    for q in range(8):
        left, right = ends[0, q : q + 1], ends[1, q : q + 1]
        result[q] = inside[q] + left * rise[q // 2] + right * fall[q // 2]
        copies.append(pltpu.make_async_copy(result.at[q], out.at[q], sem.at[q]))
        copies[-1].start()
    for copy in copies:
        copy.wait()


def local(n, rows_count, spectra, dtheta, dphi, analysis, pair_index, diffusivity):
    points, slots = spectra.shape[2], spectra.shape[3]
    radii = RADII
    halves = n * radii // points
    width = -(-dtheta.shape[1] // (128 * halves)) * 128
    extra = width * halves - dtheta.shape[1]
    if extra:
        dtheta, dphi, analysis = (jnp.pad(v, ((0, 0), (0, extra))) for v in (dtheta, dphi, analysis))
    chunks = width // 128
    vmem = pl.BlockSpec(memory_space=pltpu.VMEM)
    hbm = pl.BlockSpec(memory_space=pltpu.HBM)
    shape = spectra.shape
    table = pltpu.VMEM((chunks, slots, halves * 128), jnp.bfloat16)
    turned = pltpu.VMEM((points, 8, slots), jnp.float32)
    inside, ends, rise, fall = pl.pallas_call(
        functools.partial(step_kernel, n, rows_count),
        out_shape=(
            pltpu.VMEM((8, points, slots), jnp.float32),
            pltpu.VMEM((2, 8, slots), jnp.float32),
            pltpu.VMEM((4, points, slots), jnp.float32),
            pltpu.VMEM((4, points, slots), jnp.float32),
        ),
        in_specs=[hbm] * 6,
        out_specs=(vmem,) * 4,
        scratch_shapes=[
            pltpu.VMEM(shape, jnp.float32),
            table,
            table,
            table,
            pltpu.VMEM((chunks, n, 24 * radii, 128), jnp.bfloat16),
            pltpu.VMEM((chunks, n, 24 * radii, 128), jnp.bfloat16),
            pltpu.VMEM((6 * n + 1, 12, radii, 128), jnp.float32),
            pltpu.VMEM((chunks, n, 16 * radii, 128), jnp.bfloat16),
            pltpu.VMEM((chunks, n, 16 * radii, 128), jnp.bfloat16),
            pltpu.VMEM((rows_count, 16, slots), jnp.bfloat16),
            turned,
            turned,
            turned,
            pltpu.VMEM((2 * n, 128), jnp.int32),
            pltpu.SMEM((2 * n, 128), jnp.int32),
            pltpu.SMEM(pair_index.shape, jnp.int32),
            pltpu.SMEM(diffusivity.shape, jnp.float32),
            pltpu.SemaphoreType.DMA((3,)),
            pltpu.SemaphoreType.DMA((3, chunks, halves)),
            pltpu.SemaphoreType.DMA((1,)),
            pltpu.SemaphoreType.DMA((chunks, n)),
            pltpu.SemaphoreType.DMA((chunks, n)),
            pltpu.SemaphoreType.DMA((chunks, n)),
            pltpu.SemaphoreType.DMA((chunks, n)),
            pltpu.SemaphoreType.DMA((rows_count,)),
            pltpu.SemaphoreType.DMA((rows_count,)),
        ],
        compiler_params=pltpu.CompilerParams(
            collective_id=0, has_side_effects=True, vmem_limit_bytes=VMEM_LIMIT
        ),
        name="step",
    )(pair_index, diffusivity, spectra, dtheta, dphi, analysis)
    result = pl.pallas_call(
        finish_kernel,
        out_shape=jax.ShapeDtypeStruct((8, points, slots), jnp.float32),
        in_specs=[vmem] * 4,
        out_specs=hbm,
        scratch_shapes=[
            pltpu.VMEM((8, points, slots), jnp.float32), pltpu.SemaphoreType.DMA((8,))
        ],
        compiler_params=pltpu.CompilerParams(vmem_limit_bytes=8 * 1024 * 1024),
        name="finish",
    )(inside, ends, rise, fall)
    return result.reshape(shape)


def solution(mesh):
    n, rows_count = mesh.shape["ma"], mesh.shape["row"]
    return jax.shard_map(
        functools.partial(local, n, rows_count),
        mesh=mesh,
        in_specs=(
            P(None, None, "row", "ma"),
            P("ma", None),
            P("ma", None),
            P("ma", None),
            P(),
            P(),
        ),
        out_specs=P(None, None, "row", "ma"),
        check_vma=False,
    )
```

```python
import functools

import jax
import jax.numpy as jnp
from jax import lax
from jax.experimental import pallas as pl
from jax.experimental.pallas import tpu as pltpu
from jax.sharding import PartitionSpec as P

LMAX = 511
ROTATION = 2.0
SHELL_RADIUS = 16.0
RADII = 8
VMEM_LIMIT = 56 * 1024 * 1024
MESH = pl.DeviceIdType.MESH


def slot_rows(lowest, slots):
    slot = lax.broadcasted_iota(jnp.int32, (1, slots), 1)
    first = slot < LMAX + 1 - lowest
    held = slot < LMAX + 2
    second = jnp.logical_and(jnp.logical_not(first), held)
    degree = jnp.where(first, lowest + slot, slot - 1)
    order = jnp.where(first, lowest, LMAX - lowest)
    return first, second, held, degree, order


def say_hello(barrier, axis_sizes):
    total = 0
    for axis, size in axis_sizes:
        me = lax.axis_index(axis)
        for k in range(1, size):
            pl.semaphore_signal(
                barrier, inc=1, device_id={axis: lax.rem(me + k, size)}, device_id_type=MESH
            )
        total += size - 1
    return total


def partner_table(n, pair, out):
    count = 2 * n
    rows = lax.broadcasted_iota(jnp.int32, (count, 128), 0)
    lanes = lax.broadcasted_iota(jnp.int32, (count, 128), 1)
    values = []
    for g in range(n):
        values += [pair[g], LMAX - pair[g]]
    to = jnp.zeros((count, 128), jnp.int32)
    of = jnp.zeros((count, 128), jnp.int32)
    for k, value in enumerate(values):
        to = jnp.where(rows == k, value, to)
        of = jnp.where(lanes == k, value, of)
    need = to - of
    size = jnp.abs(need)
    place = jnp.full((count, 128), 3 * count, jnp.int32)
    for k, value in enumerate(values):
        place = jnp.where(size == value, k, place)
    place = jnp.where(jnp.logical_and(need < 0, place < count), place + count, place)
    place = jnp.where(need == of, lanes + 2 * count, place)
    out[...] = jnp.where(need > of, 3 * count, place)


def step_kernel(
    n, rows_count, pair_hbm, diffusivity_hbm, spectra_hbm, dtheta_hbm, dphi_hbm, analysis_hbm,
    local_out, ends_out, rise, fall,
    spectra, dtheta, dphi, analysis, turned_table, send, x, states, sums, got, edges, right, ahead, back,
    partner_rows, partner, pair, diffusivity,
    load_sem, piece_sem, table_sem, send_sem, recv_sem, back_send, back_recv, edge_send, edge_recv,
):
    me = lax.axis_index("ma")
    row = lax.axis_index("row")
    slots = spectra.shape[3]
    points = spectra.shape[2]
    radii = RADII
    groups = points // radii
    halves = n // groups
    chunks = dtheta.shape[0]
    width = chunks * 128
    orders = 2 * n

    def piece(i, c, h):
        source, place = ((dtheta_hbm, dtheta), (dphi_hbm, dphi), (analysis_hbm, analysis))[i]
        columns = slice(h * width + c * 128, h * width + (c + 1) * 128)
        return pltpu.make_async_copy(
            source.at[:, columns], place.at[c, :, h * 128 : (h + 1) * 128], piece_sem.at[i, c, h]
        )

    loads = [
        pltpu.make_async_copy(source, place, load_sem.at[i])
        for i, (source, place) in enumerate(
            [(pair_hbm, pair), (spectra_hbm, spectra), (diffusivity_hbm, diffusivity)]
        )
    ]
    barrier = pltpu.get_barrier_semaphore()
    greetings = say_hello(barrier, [("ma", n), ("row", rows_count)])
    loads[0].start()
    loads[1].start()
    for h in range(halves):
        piece(0, 0, h).start()
        piece(1, 0, h).start()

    def load_rest():
        for i in range(2):
            for c in range(1, chunks):
                for h in range(halves):
                    piece(i, c, h).start()
        loads[2].start()
        for c in range(chunks):
            for h in range(halves):
                piece(2, c, h).start()

    loads[0].wait()

    keep = jnp.where(pair[me] == 0, 0.0, 1.0).astype(jnp.float32)
    lowest = pair[me]
    first, second, held, degree, order = slot_rows(lowest, slots)

    loads[1].wait()
    lhs = []
    for g in range(groups):
        v = spectra[:, :, g * radii : (g + 1) * radii, :].reshape(8 * radii, slots)
        v = jnp.concatenate([jnp.where(first, v, 0.0), jnp.where(second, v, 0.0)], axis=0)
        lhs.append(v.astype(jnp.bfloat16))

    def grid_block(t, d):
        parts = []
        for j in range(2):
            z_t, w_t, s_t, a_t = (t[j, f] for f in range(4))
            z_d, w_d, s_d, a_d = (d[j, f] for f in range(4))
            pieces = [
                (w_t[0] + z_d[1], w_t[1] - z_d[0]),
                (z_t[0] - w_d[1], z_t[1] + w_d[0]),
                (s_t[0], s_t[1]),
                (-s_d[1], s_d[0]),
                (a_d[1], -a_d[0]),
                (a_t[0], a_t[1]),
            ]
            for real, imag in pieces:
                parts += [real, imag * keep if j == 0 else imag]
        return jnp.concatenate(parts, axis=0).astype(jnp.bfloat16)

    def grid_copy(e, source, c):
        return pltpu.make_async_remote_copy(
            src_ref=send.at[c, e], dst_ref=x.at[c, source],
            send_sem=send_sem.at[c, e], recv_sem=recv_sem.at[c, source],
            device_id={"ma": e}, device_id_type=MESH,
        )

    def back_copy(e, source, c):
        return pltpu.make_async_remote_copy(
            src_ref=sums.at[c, e], dst_ref=got.at[c, source],
            send_sem=back_send.at[c, e], recv_sem=back_recv.at[c, source],
            device_id={"ma": e}, device_id_type=MESH,
        )

    tall = n // 4
    my_y, my_x, my_core = me // 4, lax.rem(me // 2, 2), lax.rem(me, 2)

    def target(k):
        dy, dx, dc = k // 4, (k // 2) % 2, k % 2
        return (
            lax.rem(my_y + dy, tall) * 4 + lax.rem(my_x + dx, 2) * 2 + lax.rem(my_core + dc, 2)
        )

    for c in range(chunks):
        for h in range(halves):
            piece(0, c, h).wait()
            piece(1, c, h).wait()
        if c == 0:
            load_rest()
            for g in range(groups):
                t, d = (
                    jnp.dot(lhs[g], v[c], preferred_element_type=jnp.float32).reshape(
                        2, 4, 2, radii, halves * 128
                    )
                    for v in (dtheta, dphi)
                )
                for h in range(halves):
                    here = slice(h * 128, (h + 1) * 128)
                    send[c, g * halves + h] = grid_block(t[..., here], d[..., here])
                if g == 0:
                    pl.semaphore_wait(barrier, greetings)
                for h in range(halves):
                    e = g * halves + h

                    @pl.when(e != me)
                    def _(e=e):
                        grid_copy(e, me, 0).start()
        else:
            t, d = (
                jnp.dot(jnp.concatenate(lhs, axis=0), v[c], preferred_element_type=jnp.float32)
                for v in (dtheta, dphi)
            )
            t = t.reshape(groups, 2, 4, 2, radii, halves * 128)
            d = d.reshape(groups, 2, 4, 2, radii, halves * 128)
            for g in range(groups):
                for h in range(halves):
                    here = slice(h * 128, (h + 1) * 128)
                    send[c, g * halves + h] = grid_block(t[g, ..., here], d[g, ..., here])
            for k in range(n - 1, 0, -1):
                grid_copy(target(k), me, c).start()
        x[c, me] = send[c, me]

    partner_table(n, pair, partner_rows)
    table_copy = pltpu.make_async_copy(partner_rows, partner, table_sem.at[0])
    table_copy.start()

    near_first = sorted(range(n), key=lambda e: (e // 4 + e // 2 % 2 + e % 2, -e))

    def served(k):
        e = near_first[0]
        for at in range(1, n):
            e = jnp.where(k == at, near_first[at], e)
        return e

    alive = held.astype(jnp.float32)
    l = degree.astype(jnp.float32)
    m = order.astype(jnp.float32)
    lower = jnp.sqrt((l * l - m * m) * alive / jnp.maximum(4.0 * l * l - 1.0, 1.0)) * ROTATION
    u = l + 1.0
    upper = jnp.sqrt(jnp.maximum((u * u - m * m) / (4.0 * u * u - 1.0), 0.0))
    upper = jnp.where(degree < LMAX, upper * alive, 0.0) * ROTATION
    spin = ROTATION * m / (l * (l + 1.0) + 2.0) * alive

    loads[2].wait()
    all_points = points * rows_count
    field = lax.broadcasted_iota(jnp.int32, (8, 1), 0) // 2
    nu = jnp.zeros((8, 1), jnp.float32)
    for f in range(4):
        nu = jnp.where(field == f, diffusivity[f], nu)
    off = nu * float((all_points + 1) ** 2)
    half_excess = (1.0 + nu * (l * (l + 1.0) / SHELL_RADIUS**2)) / (2.0 * off)
    root = jnp.sqrt(half_excess * half_excess + 2.0 * half_excess)
    inverse = 1.0 + half_excess + root
    rho = 1.0 / inverse
    log_rho = -jnp.log(inverse)
    inner = alive / (2.0 * off * root)

    def power(exponent):
        return jnp.exp(log_rho * exponent)

    def couple(v):
        edge = jnp.zeros((points, 1), jnp.float32)
        below = jnp.concatenate([edge, v[:, : slots - 1]], axis=1)
        above = jnp.concatenate([v[:, 1:], edge], axis=1)
        return (lower * below + upper * above) * alive

    z0, z1 = (jnp.where(held, spectra[0, c], 0.0) for c in range(2))
    w0, w1 = (jnp.where(held, spectra[1, c], 0.0) for c in range(2))
    linear = [
        z0 - spin * z1 + couple(w0),
        z1 + spin * z0 + couple(w1),
        w0 - spin * w1 - couple(z0),
        w1 + spin * w0 - couple(z1),
    ]
    for f in (2, 3):
        for c in range(2):
            linear.append(jnp.where(held, spectra[f, c], 0.0))
    for g in range(groups):
        block = jnp.stack([v[g * radii : (g + 1) * radii] for v in linear], axis=0)
        right[g * radii : (g + 1) * radii] = jnp.swapaxes(block, 0, 1)

    at = lax.broadcasted_iota(jnp.int32, (points, slots), 0)
    for f in range(4):
        log_here = log_rho[2 * f : 2 * f + 1]
        rise[f] = jnp.exp(log_here * (at + 1).astype(jnp.float32))
        fall[f] = jnp.exp(log_here * (points - at).astype(jnp.float32))

    before = (row * points).astype(jnp.float32)
    after = ((rows_count - 1 - row) * points).astype(jnp.float32)

    zero = jnp.zeros((radii, 128), jnp.float32)
    for q in range(12):
        states[3 * orders, q] = zero
    for c in range(chunks):
        for h in range(halves):
            piece(2, c, h).wait()
        turned_table[c] = analysis[c].T
    table_copy.wait()

    def chunk_step(c, carry):
        def unpack(k, carry):
            g = target(k)

            @pl.when(k > 0)
            def _():
                grid_copy(g, g, c).wait_recv()

            block = x[c, g].astype(jnp.float32).reshape(2, 6, 2, radii, 128)
            for j in range(2):
                at_order = 2 * g + j
                u_t, u_p, s_t, s_p, b_t, b_p = (block[j, q] for q in range(6))
                for q, (p, t) in enumerate(((b_p, b_t), (u_p, u_t), (s_p, s_t))):
                    plus = (p[0] - t[1], p[1] + t[0])
                    minus = (p[0] + t[1], p[1] - t[0])
                    parts = (plus[0], plus[1], minus[0], minus[1])
                    turned = (minus[0], -minus[1], plus[0], -plus[1])
                    for i in range(4):
                        states[at_order, 4 * q + i] = parts[i]
                        states[orders + at_order, 4 * q + i] = turned[i]
                        states[2 * orders + at_order, 4 * q + i] = 0.5 * parts[i]
            return carry

        lax.fori_loop(0, n, unpack, 0)

        def one_order(i, carry):
            e = served(i // 2)
            j = lax.rem(i, 2)
            t = 2 * e + j

            def add(a, total):
                b = partner[t, a]
                vp, vm, yp, ym, wp, wm = (
                    (states[a, 2 * q], states[a, 2 * q + 1], states[b, 2 * q], states[b, 2 * q + 1])
                    for q in range(6)
                )

                def square(v):
                    ar, ai, br, bi = v
                    return ar * br - ai * bi, ar * bi + ai * br

                def cross(v, w):
                    ar, ai, br, bi = v
                    cr, ci, dr, di = w
                    return (
                        (ar * dr - ai * di) + (cr * br - ci * bi),
                        (ar * di + ai * dr) + (cr * bi + ci * br),
                    )

                terms = []
                for v, y in ((vp, yp), (vm, ym)):
                    first_term, second_term = square(v), square(y)
                    terms += [first_term[0] - second_term[0], first_term[1] - second_term[1]]
                heat, other = cross(ym, wp), cross(yp, wm)
                terms += [heat[0] + other[0], heat[1] + other[1]]
                bent, other = cross(ym, vp), cross(yp, vm)
                terms += [bent[0] - other[0], bent[1] - other[1]]
                return tuple(v + w for v, w in zip(total, terms))

            pr, pi, mr, mi, hr, hi, er, ei = lax.fori_loop(0, orders, add, (zero,) * 8, unroll=8)
            rows = [pi - mi, mr - pr, pr + mr, pi + mi, -hr, -hi, ei, -er]
            block = jnp.swapaxes(jnp.stack(rows, axis=0), 0, 1).reshape(8 * radii, 128)
            block = (0.5 * block).astype(jnp.bfloat16)
            sums[c, e, pl.ds(pl.multiple_of(j * 8 * radii, 8 * radii), 8 * radii), :] = block

            @pl.when(jnp.logical_and(j == 1, e != me))
            def _():
                back_copy(e, me, c).start()

            return carry

        lax.fori_loop(0, orders, one_order, 0)
        got[c, me] = sums[c, me]
        return carry

    lax.fori_loop(0, chunks, chunk_step, 0)

    def project(c):
        for k in range(1, n):
            e = lax.rem(me + k, n)
            back_copy(e, e, c).wait_recv()
        terms = []
        for g in range(groups):
            lhs = jnp.concatenate([got[c, g * halves + h] for h in range(halves)], axis=1)
            total = jnp.dot(lhs, turned_table[c], preferred_element_type=jnp.float32)
            total = total.reshape(2, radii, 8, slots)
            terms.append(jnp.where(first, total[0], total[1]))
        return terms

    for c in range(chunks - 1):
        for g, term in enumerate(project(c)):
            right[g * radii : (g + 1) * radii] += term
    terms = project(chunks - 1)
    source = [right[k] + terms[k // radii][k % radii] for k in range(points)]
    up, down = source[0], source[points - 1]
    ahead[0] = up
    back[points - 1] = down
    for k in range(1, points):
        up = source[k] + rho * up
        down = source[points - 1 - k] + rho * down
        ahead[k] = up
        back[points - 1 - k] = down
    edges[row] = jnp.concatenate([up, down], axis=0).astype(jnp.bfloat16)

    def edge_copy(e, source):
        return pltpu.make_async_remote_copy(
            src_ref=edges.at[row], dst_ref=edges.at[source],
            send_sem=edge_send.at[e], recv_sem=edge_recv.at[source],
            device_id={"row": e}, device_id_type=MESH,
        )

    for k in range(1, rows_count):
        edge_copy(lax.rem(row + k, rows_count), row).start()

    for g in range(groups):
        values = []
        for k in range(g * radii, (g + 1) * radii):
            value = ahead[k] + rho * back[k + 1] if k < points - 1 else ahead[k]
            values.append(inner * value)
        local_out[:, g * radii : (g + 1) * radii] = jnp.swapaxes(jnp.stack(values, axis=0), 0, 1)

    span = power(float(all_points + 1))
    scale = 1.0 / (1.0 - span * span)
    to_start, to_end = power(before), power(after)
    shifts = [power(float(k * points)) for k in range(rows_count)]
    zero = jnp.zeros((8, slots), jnp.float32)
    weights, reverses = [], []
    for e in range(rows_count):
        weight, reverse = zero, zero
        for k in range(rows_count - 1):
            weight = jnp.where(row - 1 - e == k, shifts[k], weight)
            reverse = jnp.where(e - row - 1 == k, shifts[k], reverse)
        weights.append(weight)
        reverses.append(reverse)

    for c in range(chunks):
        for k in range(1, n):
            e = lax.rem(me + k, n)
            grid_copy(e, e, c).wait_send()
            back_copy(e, e, c).wait_send()
    for k in range(1, rows_count):
        e = lax.rem(row + k, rows_count)
        edge_copy(e, e).wait()

    ahead_in, back_in, ahead_all, back_all = zero, zero, zero, zero
    for e in range(rows_count):
        both = edges[e].astype(jnp.float32)
        f_e, g_e = both[0:8], both[8:16]
        ahead_in += weights[e] * f_e
        back_in += reverses[e] * g_e
        ahead_all += shifts[rows_count - 1 - e] * f_e
        back_all += shifts[e] * g_e
    low = inner * rho * back_all
    high = inner * rho * ahead_all
    ends_out[0] = inner * ahead_in + (span * high - low) * scale * to_start
    ends_out[1] = inner * back_in + (span * low - high) * scale * to_end


def finish_kernel(inside, ends, rise, fall, out, result, sem):
    copies = []
    for q in range(8):
        left, right = ends[0, q : q + 1], ends[1, q : q + 1]
        result[q] = inside[q] + left * rise[q // 2] + right * fall[q // 2]
        copies.append(pltpu.make_async_copy(result.at[q], out.at[q], sem.at[q]))
        copies[-1].start()
    for copy in copies:
        copy.wait()


def local(n, rows_count, spectra, dtheta, dphi, analysis, pair_index, diffusivity):
    points, slots = spectra.shape[2], spectra.shape[3]
    radii = RADII
    halves = n * radii // points
    width = -(-dtheta.shape[1] // (128 * halves)) * 128
    extra = width * halves - dtheta.shape[1]
    if extra:
        dtheta, dphi, analysis = (jnp.pad(v, ((0, 0), (0, extra))) for v in (dtheta, dphi, analysis))
    chunks = width // 128
    vmem = pl.BlockSpec(memory_space=pltpu.VMEM)
    hbm = pl.BlockSpec(memory_space=pltpu.HBM)
    shape = spectra.shape
    table = pltpu.VMEM((chunks, slots, halves * 128), jnp.bfloat16)
    turned = pltpu.VMEM((points, 8, slots), jnp.float32)
    inside, ends, rise, fall = pl.pallas_call(
        functools.partial(step_kernel, n, rows_count),
        out_shape=(
            pltpu.VMEM((8, points, slots), jnp.float32),
            pltpu.VMEM((2, 8, slots), jnp.float32),
            pltpu.VMEM((4, points, slots), jnp.float32),
            pltpu.VMEM((4, points, slots), jnp.float32),
        ),
        in_specs=[hbm] * 6,
        out_specs=(vmem,) * 4,
        scratch_shapes=[
            pltpu.VMEM(shape, jnp.float32),
            table,
            table,
            table,
            pltpu.VMEM((chunks, halves * 128, slots), jnp.bfloat16),
            pltpu.VMEM((chunks, n, 24 * radii, 128), jnp.bfloat16),
            pltpu.VMEM((chunks, n, 24 * radii, 128), jnp.bfloat16),
            pltpu.VMEM((6 * n + 1, 12, radii, 128), jnp.float32),
            pltpu.VMEM((chunks, n, 16 * radii, 128), jnp.bfloat16),
            pltpu.VMEM((chunks, n, 16 * radii, 128), jnp.bfloat16),
            pltpu.VMEM((rows_count, 16, slots), jnp.bfloat16),
            turned,
            turned,
            turned,
            pltpu.VMEM((2 * n, 128), jnp.int32),
            pltpu.SMEM((2 * n, 128), jnp.int32),
            pltpu.SMEM(pair_index.shape, jnp.int32),
            pltpu.SMEM(diffusivity.shape, jnp.float32),
            pltpu.SemaphoreType.DMA((3,)),
            pltpu.SemaphoreType.DMA((3, chunks, halves)),
            pltpu.SemaphoreType.DMA((1,)),
            pltpu.SemaphoreType.DMA((chunks, n)),
            pltpu.SemaphoreType.DMA((chunks, n)),
            pltpu.SemaphoreType.DMA((chunks, n)),
            pltpu.SemaphoreType.DMA((chunks, n)),
            pltpu.SemaphoreType.DMA((rows_count,)),
            pltpu.SemaphoreType.DMA((rows_count,)),
        ],
        compiler_params=pltpu.CompilerParams(
            collective_id=0, has_side_effects=True, vmem_limit_bytes=VMEM_LIMIT
        ),
        name="step",
    )(pair_index, diffusivity, spectra, dtheta, dphi, analysis)
    result = pl.pallas_call(
        finish_kernel,
        out_shape=jax.ShapeDtypeStruct((8, points, slots), jnp.float32),
        in_specs=[vmem] * 4,
        out_specs=hbm,
        scratch_shapes=[
            pltpu.VMEM((8, points, slots), jnp.float32), pltpu.SemaphoreType.DMA((8,))
        ],
        compiler_params=pltpu.CompilerParams(vmem_limit_bytes=8 * 1024 * 1024),
        name="finish",
    )(inside, ends, rise, fall)
    return result.reshape(shape)


def solution(mesh):
    n, rows_count = mesh.shape["ma"], mesh.shape["row"]
    return jax.shard_map(
        functools.partial(local, n, rows_count),
        mesh=mesh,
        in_specs=(
            P(None, None, "row", "ma"),
            P("ma", None),
            P("ma", None),
            P("ma", None),
            P(),
            P(),
        ),
        out_specs=P(None, None, "row", "ma"),
        check_vma=False,
    )
```

```python
import functools

import jax
import jax.numpy as jnp
from jax import lax
from jax.experimental import pallas as pl
from jax.experimental.pallas import tpu as pltpu
from jax.sharding import PartitionSpec as P

LMAX = 511
ROTATION = 2.0
SHELL_RADIUS = 16.0
RADII = 8
VMEM_LIMIT = 56 * 1024 * 1024
MESH = pl.DeviceIdType.MESH


def slot_rows(lowest, slots):
    slot = lax.broadcasted_iota(jnp.int32, (1, slots), 1)
    first = slot < LMAX + 1 - lowest
    held = slot < LMAX + 2
    second = jnp.logical_and(jnp.logical_not(first), held)
    degree = jnp.where(first, lowest + slot, slot - 1)
    order = jnp.where(first, lowest, LMAX - lowest)
    return first, second, held, degree, order


def say_hello(barrier, n, rows_count, me, row):
    def greet(**device):
        pl.semaphore_signal(barrier, inc=1, device_id=device, device_id_type=MESH)

    @pl.when(me >= 2)
    def _():
        greet(ma=0)
        greet(ma=1)

    @pl.when(me < 2)
    def _():
        for e in range(2, n):
            greet(ma=e)
        greet(ma=1 - me)

    @pl.when(me == 0)
    def _():
        for k in range(1, rows_count):
            greet(row=lax.rem(row + k, rows_count))

    return jnp.where(me == 0, n - 1 + rows_count - 1, jnp.where(me == 1, n - 1, 2))


def partner_table(n, pair, out):
    count = 2 * n
    rows = lax.broadcasted_iota(jnp.int32, (count, 128), 0)
    lanes = lax.broadcasted_iota(jnp.int32, (count, 128), 1)
    values = []
    for g in range(n):
        values += [pair[g], LMAX - pair[g]]
    to = jnp.zeros((count, 128), jnp.int32)
    of = jnp.zeros((count, 128), jnp.int32)
    for k, value in enumerate(values):
        to = jnp.where(rows == k, value, to)
        of = jnp.where(lanes == k, value, of)
    need = to - of
    size = jnp.abs(need)
    place = jnp.full((count, 128), 3 * count, jnp.int32)
    for k, value in enumerate(values):
        place = jnp.where(size == value, k, place)
    place = jnp.where(jnp.logical_and(need < 0, place < count), place + count, place)
    place = jnp.where(need == of, lanes + 2 * count, place)
    out[...] = jnp.where(need > of, 3 * count, place)


def step_kernel(
    n, rows_count, pair_hbm, diffusivity_hbm, spectra_hbm, dtheta_hbm, dphi_hbm, analysis_hbm,
    local_out, ends_out, rise, fall,
    spectra, dtheta, dphi, analysis, turned_table, send, x, states, sums, got, edges, right, ahead, back,
    partner_rows, partner, pair, diffusivity,
    load_sem, piece_sem, table_sem, send_sem, recv_sem, back_send, back_recv, edge_send, edge_recv,
    plane_sem, planes_sem, rows_sem,
):
    me = lax.axis_index("ma")
    row = lax.axis_index("row")
    slots = spectra.shape[3]
    points = spectra.shape[2]
    radii = RADII
    groups = points // radii
    halves = n // groups
    chunks = dtheta.shape[0]
    width = chunks * 128
    orders = 2 * n

    def piece(i, c, h):
        source, place = ((dtheta_hbm, dtheta), (dphi_hbm, dphi), (analysis_hbm, analysis))[i]
        columns = slice(h * width + c * 128, h * width + (c + 1) * 128)
        return pltpu.make_async_copy(
            source.at[:, columns], place.at[c, :, h * 128 : (h + 1) * 128], piece_sem.at[i, c, h]
        )

    loads = [
        pltpu.make_async_copy(source, place, load_sem.at[i])
        for i, (source, place) in enumerate(
            [(pair_hbm, pair), (diffusivity_hbm, diffusivity)]
            + [
                (
                    spectra_hbm.at[:, :, g * radii : (g + 1) * radii],
                    spectra.at[:, :, g * radii : (g + 1) * radii],
                )
                for g in range(groups)
            ]
        )
    ]
    loads[0].start()
    loads[2].start()
    for h in range(halves):
        piece(0, 0, h).start()
        piece(1, 0, h).start()
    for g in range(1, groups):
        loads[2 + g].start()

    barrier = pltpu.get_barrier_semaphore()
    greetings = say_hello(barrier, n, rows_count, me, row)

    def load_rest():
        for i in range(2):
            for c in range(1, chunks):
                for h in range(halves):
                    piece(i, c, h).start()
        loads[1].start()
        for c in range(chunks):
            for h in range(halves):
                piece(2, c, h).start()

    loads[0].wait()

    keep = jnp.where(pair[me] == 0, 0.0, 1.0).astype(jnp.float32)
    lowest = pair[me]
    first, second, held, degree, order = slot_rows(lowest, slots)

    def group_rows(g):
        v = spectra[:, :, g * radii : (g + 1) * radii, :].reshape(8 * radii, slots)
        v = jnp.concatenate([jnp.where(first, v, 0.0), jnp.where(second, v, 0.0)], axis=0)
        return v.astype(jnp.bfloat16)

    lhs = []

    def grid_block(t, d):
        parts = []
        for j in range(2):
            z_t, w_t, s_t, a_t = (t[j, f] for f in range(4))
            z_d, w_d, s_d, a_d = (d[j, f] for f in range(4))
            pieces = [
                (w_t[0] + z_d[1], w_t[1] - z_d[0]),
                (z_t[0] - w_d[1], z_t[1] + w_d[0]),
                (s_t[0], s_t[1]),
                (-s_d[1], s_d[0]),
                (a_d[1], -a_d[0]),
                (a_t[0], a_t[1]),
            ]
            for real, imag in pieces:
                parts += [real, imag * keep if j == 0 else imag]
        return jnp.concatenate(parts, axis=0).astype(jnp.bfloat16)

    def grid_copy(e, source, c):
        return pltpu.make_async_remote_copy(
            src_ref=send.at[c, e], dst_ref=x.at[c, source],
            send_sem=send_sem.at[c, e], recv_sem=recv_sem.at[c, source],
            device_id={"ma": e}, device_id_type=MESH,
        )

    def back_copy(e, source, c):
        return pltpu.make_async_remote_copy(
            src_ref=sums.at[c, e], dst_ref=got.at[c, source],
            send_sem=back_send.at[c, e], recv_sem=back_recv.at[c, source],
            device_id={"ma": e}, device_id_type=MESH,
        )

    def tell(sem, **device):
        pl.semaphore_signal(sem, inc=1, device_id=device, device_id_type=MESH)

    tall = n // 4
    my_y, my_x, my_core = me // 4, lax.rem(me // 2, 2), lax.rem(me, 2)

    def target(k):
        dy, dx, dc = k // 4, (k // 2) % 2, k % 2
        return (
            lax.rem(my_y + dy, tall) * 4 + lax.rem(my_x + dx, 2) * 2 + lax.rem(my_core + dc, 2)
        )

    for c in range(chunks):
        for h in range(halves):
            piece(0, c, h).wait()
            piece(1, c, h).wait()
        if c == 0:
            load_rest()
            for g in range(groups):
                loads[2 + g].wait()
                lhs.append(group_rows(g))
                t, d = (
                    jnp.dot(lhs[g], v[c], preferred_element_type=jnp.float32).reshape(
                        2, 4, 2, radii, halves * 128
                    )
                    for v in (dtheta, dphi)
                )
                for h in range(halves):
                    here = slice(h * 128, (h + 1) * 128)
                    send[c, g * halves + h] = grid_block(t[..., here], d[..., here])
                if g == 0:
                    pl.semaphore_wait(barrier, greetings)

                    @pl.when(me == 0)
                    def _():
                        for e in range(2, n):
                            tell(plane_sem, ma=e)
                        for k in range(1, rows_count):
                            tell(planes_sem, row=lax.rem(row + k, rows_count))

                for h in range(halves):
                    e = g * halves + h
                    if e == 2:

                        @pl.when(me >= 2)
                        def _():
                            pl.semaphore_wait(plane_sem, 1)


                    @pl.when(e != me)
                    def _(e=e):
                        grid_copy(e, me, 0).start()
        else:
            t, d = (
                jnp.dot(jnp.concatenate(lhs, axis=0), v[c], preferred_element_type=jnp.float32)
                for v in (dtheta, dphi)
            )
            t = t.reshape(groups, 2, 4, 2, radii, halves * 128)
            d = d.reshape(groups, 2, 4, 2, radii, halves * 128)
            for g in range(groups):
                for h in range(halves):
                    here = slice(h * 128, (h + 1) * 128)
                    send[c, g * halves + h] = grid_block(t[g, ..., here], d[g, ..., here])
            for e in range(n):

                @pl.when(e != me)
                def _(e=e, c=c):
                    grid_copy(e, me, c).start()


    partner_table(n, pair, partner_rows)
    table_copy = pltpu.make_async_copy(partner_rows, partner, table_sem.at[0])
    table_copy.start()

    for c in range(chunks):
        x[c, me] = send[c, me]

    near_first = sorted(range(n), key=lambda e: (e // 4 + e // 2 % 2 + e % 2, -e))

    def served(k):
        e = near_first[0]
        for at in range(1, n):
            e = jnp.where(k == at, near_first[at], e)
        return e

    alive = held.astype(jnp.float32)
    l = degree.astype(jnp.float32)
    m = order.astype(jnp.float32)
    lower = jnp.sqrt((l * l - m * m) * alive / jnp.maximum(4.0 * l * l - 1.0, 1.0)) * ROTATION
    u = l + 1.0
    upper = jnp.sqrt(jnp.maximum((u * u - m * m) / (4.0 * u * u - 1.0), 0.0))
    upper = jnp.where(degree < LMAX, upper * alive, 0.0) * ROTATION
    spin = ROTATION * m / (l * (l + 1.0) + 2.0) * alive

    loads[1].wait()
    all_points = points * rows_count
    field = lax.broadcasted_iota(jnp.int32, (8, 1), 0) // 2
    nu = jnp.zeros((8, 1), jnp.float32)
    for f in range(4):
        nu = jnp.where(field == f, diffusivity[f], nu)
    off = nu * float((all_points + 1) ** 2)
    half_excess = (1.0 + nu * (l * (l + 1.0) / SHELL_RADIUS**2)) / (2.0 * off)
    root = jnp.sqrt(half_excess * half_excess + 2.0 * half_excess)
    inverse = 1.0 + half_excess + root
    rho = 1.0 / inverse
    log_rho = -jnp.log(inverse)
    inner = alive / (2.0 * off * root)

    def power(exponent):
        return jnp.exp(log_rho * exponent)

    def couple(v):
        edge = jnp.zeros((points, 1), jnp.float32)
        below = jnp.concatenate([edge, v[:, : slots - 1]], axis=1)
        above = jnp.concatenate([v[:, 1:], edge], axis=1)
        return (lower * below + upper * above) * alive

    z0, z1 = (jnp.where(held, spectra[0, c], 0.0) for c in range(2))
    w0, w1 = (jnp.where(held, spectra[1, c], 0.0) for c in range(2))
    linear = [
        z0 - spin * z1 + couple(w0),
        z1 + spin * z0 + couple(w1),
        w0 - spin * w1 - couple(z0),
        w1 + spin * w0 - couple(z1),
    ]
    for f in (2, 3):
        for c in range(2):
            linear.append(jnp.where(held, spectra[f, c], 0.0))
    for g in range(groups):
        block = jnp.stack([v[g * radii : (g + 1) * radii] for v in linear], axis=0)
        right[g * radii : (g + 1) * radii] = jnp.swapaxes(block, 0, 1)

    at = lax.broadcasted_iota(jnp.int32, (points, slots), 0)
    for f in range(4):
        log_here = log_rho[2 * f : 2 * f + 1]
        rise[f] = jnp.exp(log_here * (at + 1).astype(jnp.float32))
        fall[f] = jnp.exp(log_here * (points - at).astype(jnp.float32))

    before = (row * points).astype(jnp.float32)
    after = ((rows_count - 1 - row) * points).astype(jnp.float32)

    zero = jnp.zeros((radii, 128), jnp.float32)
    for q in range(12):
        states[3 * orders, q] = zero
    for c in range(chunks):
        for h in range(halves):
            piece(2, c, h).wait()
        turned_table[c] = analysis[c].T
    table_copy.wait()

    @pl.when(me == 0)
    def _():
        pl.semaphore_wait(planes_sem, rows_count - 1)
        for e in range(1, n):
            tell(rows_sem, ma=e)

    def chunk_step(c, carry):
        def unpack(k, carry):
            g = target(k)

            @pl.when(k > 0)
            def _():
                grid_copy(g, g, c).wait_recv()

            block = x[c, g].astype(jnp.float32).reshape(2, 6, 2, radii, 128)
            for j in range(2):
                at_order = 2 * g + j
                u_t, u_p, s_t, s_p, b_t, b_p = (block[j, q] for q in range(6))
                for q, (p, t) in enumerate(((b_p, b_t), (u_p, u_t), (s_p, s_t))):
                    plus = (p[0] - t[1], p[1] + t[0])
                    minus = (p[0] + t[1], p[1] - t[0])
                    parts = (plus[0], plus[1], minus[0], minus[1])
                    turned = (minus[0], -minus[1], plus[0], -plus[1])
                    for i in range(4):
                        states[at_order, 4 * q + i] = parts[i]
                        states[orders + at_order, 4 * q + i] = turned[i]
                        states[2 * orders + at_order, 4 * q + i] = 0.5 * parts[i]
            return carry

        lax.fori_loop(0, n, unpack, 0)

        def one_order(i, carry):
            e = served(i // 2)
            j = lax.rem(i, 2)
            t = 2 * e + j

            def add(a, total):
                b = partner[t, a]
                vp, vm, yp, ym, wp, wm = (
                    (states[a, 2 * q], states[a, 2 * q + 1], states[b, 2 * q], states[b, 2 * q + 1])
                    for q in range(6)
                )

                def square(v):
                    ar, ai, br, bi = v
                    return ar * br - ai * bi, ar * bi + ai * br

                def cross(v, w):
                    ar, ai, br, bi = v
                    cr, ci, dr, di = w
                    return (
                        (ar * dr - ai * di) + (cr * br - ci * bi),
                        (ar * di + ai * dr) + (cr * bi + ci * br),
                    )

                terms = []
                for v, y in ((vp, yp), (vm, ym)):
                    first_term, second_term = square(v), square(y)
                    terms += [first_term[0] - second_term[0], first_term[1] - second_term[1]]
                heat, other = cross(ym, wp), cross(yp, wm)
                terms += [heat[0] + other[0], heat[1] + other[1]]
                bent, other = cross(ym, vp), cross(yp, vm)
                terms += [bent[0] - other[0], bent[1] - other[1]]
                return tuple(v + w for v, w in zip(total, terms))

            pr, pi, mr, mi, hr, hi, er, ei = lax.fori_loop(0, orders, add, (zero,) * 8, unroll=8)
            rows = [pi - mi, mr - pr, pr + mr, pi + mi, -hr, -hi, ei, -er]
            block = jnp.swapaxes(jnp.stack(rows, axis=0), 0, 1).reshape(8 * radii, 128)
            block = (0.5 * block).astype(jnp.bfloat16)
            sums[c, e, pl.ds(pl.multiple_of(j * 8 * radii, 8 * radii), 8 * radii), :] = block

            @pl.when(jnp.logical_and(j == 1, e != me))
            def _():
                back_copy(e, me, c).start()

            return carry

        lax.fori_loop(0, orders, one_order, 0)
        got[c, me] = sums[c, me]
        return carry

    lax.fori_loop(0, chunks, chunk_step, 0)

    def project(c):
        for k in range(1, n):
            e = lax.rem(me + k, n)
            back_copy(e, e, c).wait_recv()
        terms = []
        for g in range(groups):
            lhs = jnp.concatenate([got[c, g * halves + h] for h in range(halves)], axis=1)
            total = jnp.dot(lhs, turned_table[c], preferred_element_type=jnp.float32)
            total = total.reshape(2, radii, 8, slots)
            terms.append(jnp.where(first, total[0], total[1]))
        return terms

    for c in range(chunks - 1):
        for g, term in enumerate(project(c)):
            right[g * radii : (g + 1) * radii] += term
    terms = project(chunks - 1)
    source = [right[k] + terms[k // radii][k % radii] for k in range(points)]
    up, down = source[0], source[points - 1]
    ahead[0] = up
    back[points - 1] = down
    for k in range(1, points):
        up = source[k] + rho * up
        down = source[points - 1 - k] + rho * down
        ahead[k] = up
        back[points - 1 - k] = down
    @pl.when(me > 0)
    def _():
        pl.semaphore_wait(rows_sem, 1)

    edges[row] = jnp.concatenate([up, down], axis=0).astype(jnp.bfloat16)

    def edge_copy(e, source):
        return pltpu.make_async_remote_copy(
            src_ref=edges.at[row], dst_ref=edges.at[source],
            send_sem=edge_send.at[e], recv_sem=edge_recv.at[source],
            device_id={"row": e}, device_id_type=MESH,
        )

    for k in range(1, rows_count):
        edge_copy(lax.rem(row + k, rows_count), row).start()

    for g in range(groups):
        values = []
        for k in range(g * radii, (g + 1) * radii):
            value = ahead[k] + rho * back[k + 1] if k < points - 1 else ahead[k]
            values.append(inner * value)
        local_out[:, g * radii : (g + 1) * radii] = jnp.swapaxes(jnp.stack(values, axis=0), 0, 1)

    span = power(float(all_points + 1))
    scale = 1.0 / (1.0 - span * span)
    to_start, to_end = power(before), power(after)
    shifts = [power(float(k * points)) for k in range(rows_count)]
    zero = jnp.zeros((8, slots), jnp.float32)
    weights, reverses = [], []
    for e in range(rows_count):
        weight, reverse = zero, zero
        for k in range(rows_count - 1):
            weight = jnp.where(row - 1 - e == k, shifts[k], weight)
            reverse = jnp.where(e - row - 1 == k, shifts[k], reverse)
        weights.append(weight)
        reverses.append(reverse)

    for c in range(chunks):
        for k in range(1, n):
            e = lax.rem(me + k, n)
            grid_copy(e, e, c).wait_send()
            back_copy(e, e, c).wait_send()
    for k in range(1, rows_count):
        e = lax.rem(row + k, rows_count)
        edge_copy(e, e).wait()

    ahead_in, back_in, ahead_all, back_all = zero, zero, zero, zero
    for e in range(rows_count):
        both = edges[e].astype(jnp.float32)
        f_e, g_e = both[0:8], both[8:16]
        ahead_in += weights[e] * f_e
        back_in += reverses[e] * g_e
        ahead_all += shifts[rows_count - 1 - e] * f_e
        back_all += shifts[e] * g_e
    low = inner * rho * back_all
    high = inner * rho * ahead_all
    ends_out[0] = inner * ahead_in + (span * high - low) * scale * to_start
    ends_out[1] = inner * back_in + (span * low - high) * scale * to_end


def finish_kernel(inside, ends, rise, fall, out, result, sem):
    copies = []
    for q in range(8):
        left, right = ends[0, q : q + 1], ends[1, q : q + 1]
        result[q] = inside[q] + left * rise[q // 2] + right * fall[q // 2]
        copies.append(pltpu.make_async_copy(result.at[q], out.at[q], sem.at[q]))
        copies[-1].start()
    for copy in copies:
        copy.wait()


def local(n, rows_count, spectra, dtheta, dphi, analysis, pair_index, diffusivity):
    points, slots = spectra.shape[2], spectra.shape[3]
    radii = RADII
    halves = n * radii // points
    width = -(-dtheta.shape[1] // (128 * halves)) * 128
    extra = width * halves - dtheta.shape[1]
    if extra:
        dtheta, dphi, analysis = (jnp.pad(v, ((0, 0), (0, extra))) for v in (dtheta, dphi, analysis))
    chunks = width // 128
    vmem = pl.BlockSpec(memory_space=pltpu.VMEM)
    hbm = pl.BlockSpec(memory_space=pltpu.HBM)
    shape = spectra.shape
    table = pltpu.VMEM((chunks, slots, halves * 128), jnp.bfloat16)
    turned = pltpu.VMEM((points, 8, slots), jnp.float32)
    inside, ends, rise, fall = pl.pallas_call(
        functools.partial(step_kernel, n, rows_count),
        out_shape=(
            pltpu.VMEM((8, points, slots), jnp.float32),
            pltpu.VMEM((2, 8, slots), jnp.float32),
            pltpu.VMEM((4, points, slots), jnp.float32),
            pltpu.VMEM((4, points, slots), jnp.float32),
        ),
        in_specs=[hbm] * 6,
        out_specs=(vmem,) * 4,
        scratch_shapes=[
            pltpu.VMEM(shape, jnp.float32),
            table,
            table,
            table,
            pltpu.VMEM((chunks, halves * 128, slots), jnp.bfloat16),
            pltpu.VMEM((chunks, n, 24 * radii, 128), jnp.bfloat16),
            pltpu.VMEM((chunks, n, 24 * radii, 128), jnp.bfloat16),
            pltpu.VMEM((6 * n + 1, 12, radii, 128), jnp.float32),
            pltpu.VMEM((chunks, n, 16 * radii, 128), jnp.bfloat16),
            pltpu.VMEM((chunks, n, 16 * radii, 128), jnp.bfloat16),
            pltpu.VMEM((rows_count, 16, slots), jnp.bfloat16),
            turned,
            turned,
            turned,
            pltpu.VMEM((2 * n, 128), jnp.int32),
            pltpu.SMEM((2 * n, 128), jnp.int32),
            pltpu.SMEM(pair_index.shape, jnp.int32),
            pltpu.SMEM(diffusivity.shape, jnp.float32),
            pltpu.SemaphoreType.DMA((2 + points // radii,)),
            pltpu.SemaphoreType.DMA((3, chunks, halves)),
            pltpu.SemaphoreType.DMA((1,)),
            pltpu.SemaphoreType.DMA((chunks, n)),
            pltpu.SemaphoreType.DMA((chunks, n)),
            pltpu.SemaphoreType.DMA((chunks, n)),
            pltpu.SemaphoreType.DMA((chunks, n)),
            pltpu.SemaphoreType.DMA((rows_count,)),
            pltpu.SemaphoreType.DMA((rows_count,)),
            pltpu.SemaphoreType.REGULAR,
            pltpu.SemaphoreType.REGULAR,
            pltpu.SemaphoreType.REGULAR,
        ],
        compiler_params=pltpu.CompilerParams(
            collective_id=0, has_side_effects=True, vmem_limit_bytes=VMEM_LIMIT
        ),
        name="step",
    )(pair_index, diffusivity, spectra, dtheta, dphi, analysis)
    result = pl.pallas_call(
        finish_kernel,
        out_shape=jax.ShapeDtypeStruct((8, points, slots), jnp.float32),
        in_specs=[vmem] * 4,
        out_specs=hbm,
        scratch_shapes=[
            pltpu.VMEM((8, points, slots), jnp.float32), pltpu.SemaphoreType.DMA((8,))
        ],
        compiler_params=pltpu.CompilerParams(vmem_limit_bytes=8 * 1024 * 1024),
        name="finish",
    )(inside, ends, rise, fall)
    return result.reshape(shape)


def solution(mesh):
    n, rows_count = mesh.shape["ma"], mesh.shape["row"]
    return jax.shard_map(
        functools.partial(local, n, rows_count),
        mesh=mesh,
        in_specs=(
            P(None, None, "row", "ma"),
            P("ma", None),
            P("ma", None),
            P("ma", None),
            P(),
            P(),
        ),
        out_specs=P(None, None, "row", "ma"),
        check_vma=False,
    )
```

```python
import functools

import jax
import jax.numpy as jnp
from jax import lax
from jax.experimental import pallas as pl
from jax.experimental.pallas import tpu as pltpu
from jax.sharding import PartitionSpec as P

LMAX = 511
ROTATION = 2.0
SHELL_RADIUS = 16.0
RADII = 8
VMEM_LIMIT = 56 * 1024 * 1024
MESH = pl.DeviceIdType.MESH


def slot_rows(lowest, slots):
    slot = lax.broadcasted_iota(jnp.int32, (1, slots), 1)
    first = slot < LMAX + 1 - lowest
    held = slot < LMAX + 2
    second = jnp.logical_and(jnp.logical_not(first), held)
    degree = jnp.where(first, lowest + slot, slot - 1)
    order = jnp.where(first, lowest, LMAX - lowest)
    return first, second, held, degree, order


def say_hello(barrier, n, rows_count, me, row):
    def greet(**device):
        pl.semaphore_signal(barrier, inc=1, device_id=device, device_id_type=MESH)

    @pl.when(me >= 2)
    def _():
        greet(ma=0)
        greet(ma=1)

    @pl.when(me < 2)
    def _():
        for e in range(2, n):
            greet(ma=e)
        greet(ma=1 - me)

    @pl.when(me == 0)
    def _():
        for k in range(1, rows_count):
            greet(row=lax.rem(row + k, rows_count))

    return jnp.where(me == 0, n - 1 + rows_count - 1, jnp.where(me == 1, n - 1, 2))


def partner_table(n, pair, out):
    count = 2 * n
    rows = lax.broadcasted_iota(jnp.int32, (count, 128), 0)
    lanes = lax.broadcasted_iota(jnp.int32, (count, 128), 1)
    values = []
    for g in range(n):
        values += [pair[g], LMAX - pair[g]]
    to = jnp.zeros((count, 128), jnp.int32)
    of = jnp.zeros((count, 128), jnp.int32)
    for k, value in enumerate(values):
        to = jnp.where(rows == k, value, to)
        of = jnp.where(lanes == k, value, of)
    need = to - of
    size = jnp.abs(need)
    place = jnp.full((count, 128), 3 * count, jnp.int32)
    for k, value in enumerate(values):
        place = jnp.where(size == value, k, place)
    place = jnp.where(jnp.logical_and(need < 0, place < count), place + count, place)
    place = jnp.where(need == of, lanes + 2 * count, place)
    out[...] = jnp.where(need > of, 3 * count, place)


def step_kernel(
    n, rows_count, pair_hbm, diffusivity_hbm, spectra_hbm, dtheta_hbm, dphi_hbm, analysis_hbm,
    local_out, ends_out, rise, fall,
    spectra, dtheta, dphi, analysis, turned_table, send, x, states, sums, got, edges, right, ahead, back,
    partner_rows, partner, pair, diffusivity,
    load_sem, piece_sem, table_sem, send_sem, recv_sem, back_send, back_recv, edge_send, edge_recv,
    plane_sem, planes_sem, rows_sem,
):
    me = lax.axis_index("ma")
    row = lax.axis_index("row")
    slots = spectra.shape[3]
    points = spectra.shape[2]
    radii = RADII
    groups = points // radii
    halves = n // groups
    chunks = dtheta.shape[0]
    width = chunks * 128
    orders = 2 * n

    def piece(i, c, h):
        source, place = ((dtheta_hbm, dtheta), (dphi_hbm, dphi), (analysis_hbm, analysis))[i]
        columns = slice(h * width + c * 128, h * width + (c + 1) * 128)
        return pltpu.make_async_copy(
            source.at[:, columns], place.at[c, :, h * 128 : (h + 1) * 128], piece_sem.at[i, c, h]
        )

    loads = [
        pltpu.make_async_copy(source, place, load_sem.at[i])
        for i, (source, place) in enumerate(
            [(pair_hbm, pair), (diffusivity_hbm, diffusivity)]
            + [
                (
                    spectra_hbm.at[:, :, g * radii : (g + 1) * radii],
                    spectra.at[:, :, g * radii : (g + 1) * radii],
                )
                for g in range(groups)
            ]
        )
    ]
    loads[0].start()
    loads[2].start()
    for h in range(halves):
        piece(0, 0, h).start()
        piece(1, 0, h).start()
    for g in range(1, groups):
        loads[2 + g].start()

    barrier = pltpu.get_barrier_semaphore()
    greetings = say_hello(barrier, n, rows_count, me, row)

    def load_rest():
        for i in range(2):
            for c in range(1, chunks):
                for h in range(halves):
                    piece(i, c, h).start()
        loads[1].start()
        for c in range(chunks):
            for h in range(halves):
                piece(2, c, h).start()

    loads[0].wait()

    keep = jnp.where(pair[me] == 0, 0.0, 1.0).astype(jnp.float32)
    lowest = pair[me]
    first, second, held, degree, order = slot_rows(lowest, slots)

    def group_rows(g):
        v = spectra[:, :, g * radii : (g + 1) * radii, :].reshape(8 * radii, slots)
        v = jnp.concatenate([jnp.where(first, v, 0.0), jnp.where(second, v, 0.0)], axis=0)
        return v.astype(jnp.bfloat16)

    lhs = []

    def grid_block(t, d):
        parts = []
        for j in range(2):
            z_t, w_t, s_t, a_t = (t[j, f] for f in range(4))
            z_d, w_d, s_d, a_d = (d[j, f] for f in range(4))
            pieces = [
                (w_t[0] + z_d[1], w_t[1] - z_d[0]),
                (z_t[0] - w_d[1], z_t[1] + w_d[0]),
                (s_t[0], s_t[1]),
                (-s_d[1], s_d[0]),
                (a_d[1], -a_d[0]),
                (a_t[0], a_t[1]),
            ]
            for real, imag in pieces:
                parts += [real, imag * keep if j == 0 else imag]
        return jnp.concatenate(parts, axis=0).astype(jnp.bfloat16)

    def grid_copy(e, source, c):
        return pltpu.make_async_remote_copy(
            src_ref=send.at[c, e], dst_ref=x.at[c, source],
            send_sem=send_sem.at[c, e], recv_sem=recv_sem.at[c, source],
            device_id={"ma": e}, device_id_type=MESH,
        )

    def back_copy(e, source, c):
        return pltpu.make_async_remote_copy(
            src_ref=sums.at[c, e], dst_ref=got.at[c, source],
            send_sem=back_send.at[c, e], recv_sem=back_recv.at[c, source],
            device_id={"ma": e}, device_id_type=MESH,
        )

    def tell(sem, **device):
        pl.semaphore_signal(sem, inc=1, device_id=device, device_id_type=MESH)

    tall = n // 4
    my_y, my_x, my_core = me // 4, lax.rem(me // 2, 2), lax.rem(me, 2)

    def target(k):
        dy, dx, dc = k // 4, (k // 2) % 2, k % 2
        return (
            lax.rem(my_y + dy, tall) * 4 + lax.rem(my_x + dx, 2) * 2 + lax.rem(my_core + dc, 2)
        )

    for c in range(chunks):
        for h in range(halves):
            piece(0, c, h).wait()
            piece(1, c, h).wait()
        if c == 0:
            load_rest()
            for g in range(groups):
                loads[2 + g].wait()
                lhs.append(group_rows(g))
                t, d = (
                    jnp.dot(lhs[g], v[c], preferred_element_type=jnp.float32).reshape(
                        2, 4, 2, radii, halves * 128
                    )
                    for v in (dtheta, dphi)
                )
                for h in range(halves):
                    here = slice(h * 128, (h + 1) * 128)
                    send[c, g * halves + h] = grid_block(t[..., here], d[..., here])
                if g == 0:
                    pl.semaphore_wait(barrier, greetings)

                    @pl.when(me == 0)
                    def _():
                        for e in range(2, n):
                            tell(plane_sem, ma=e)
                        for k in range(1, rows_count):
                            tell(planes_sem, row=lax.rem(row + k, rows_count))

                for h in range(halves):
                    e = g * halves + h
                    if e == 2:

                        @pl.when(me >= 2)
                        def _():
                            pl.semaphore_wait(plane_sem, 1)


                    @pl.when(e != me)
                    def _(e=e):
                        grid_copy(e, me, 0).start()
        else:
            t, d = (
                jnp.dot(jnp.concatenate(lhs, axis=0), v[c], preferred_element_type=jnp.float32)
                for v in (dtheta, dphi)
            )
            t = t.reshape(groups, 2, 4, 2, radii, halves * 128)
            d = d.reshape(groups, 2, 4, 2, radii, halves * 128)
            for g in range(groups):
                for h in range(halves):
                    here = slice(h * 128, (h + 1) * 128)
                    send[c, g * halves + h] = grid_block(t[g, ..., here], d[g, ..., here])
            for e in range(n):

                @pl.when(e != me)
                def _(e=e, c=c):
                    grid_copy(e, me, c).start()


    partner_table(n, pair, partner_rows)
    table_copy = pltpu.make_async_copy(partner_rows, partner, table_sem.at[0])
    table_copy.start()

    for c in range(chunks):
        x[c, me] = send[c, me]

    near_first = sorted(range(n), key=lambda e: (e // 4 + e // 2 % 2 + e % 2, -e))

    def served(k):
        e = near_first[0]
        for at in range(1, n):
            e = jnp.where(k == at, near_first[at], e)
        return e

    alive = held.astype(jnp.float32)
    l = degree.astype(jnp.float32)
    m = order.astype(jnp.float32)
    lower = jnp.sqrt((l * l - m * m) * alive / jnp.maximum(4.0 * l * l - 1.0, 1.0)) * ROTATION
    u = l + 1.0
    upper = jnp.sqrt(jnp.maximum((u * u - m * m) / (4.0 * u * u - 1.0), 0.0))
    upper = jnp.where(degree < LMAX, upper * alive, 0.0) * ROTATION
    spin = ROTATION * m / (l * (l + 1.0) + 2.0) * alive

    loads[1].wait()
    all_points = points * rows_count
    field = lax.broadcasted_iota(jnp.int32, (8, 1), 0) // 2
    nu = jnp.zeros((8, 1), jnp.float32)
    for f in range(4):
        nu = jnp.where(field == f, diffusivity[f], nu)
    off = nu * float((all_points + 1) ** 2)
    half_excess = (1.0 + nu * (l * (l + 1.0) / SHELL_RADIUS**2)) / (2.0 * off)
    root = jnp.sqrt(half_excess * half_excess + 2.0 * half_excess)
    inverse = 1.0 + half_excess + root
    rho = 1.0 / inverse
    log_rho = -jnp.log(inverse)
    inner = alive / (2.0 * off * root)

    def power(exponent):
        return jnp.exp(log_rho * exponent)

    def couple(v):
        edge = jnp.zeros((points, 1), jnp.float32)
        below = jnp.concatenate([edge, v[:, : slots - 1]], axis=1)
        above = jnp.concatenate([v[:, 1:], edge], axis=1)
        return (lower * below + upper * above) * alive

    z0, z1 = (jnp.where(held, spectra[0, c], 0.0) for c in range(2))
    w0, w1 = (jnp.where(held, spectra[1, c], 0.0) for c in range(2))
    linear = [
        z0 - spin * z1 + couple(w0),
        z1 + spin * z0 + couple(w1),
        w0 - spin * w1 - couple(z0),
        w1 + spin * w0 - couple(z1),
    ]
    for f in (2, 3):
        for c in range(2):
            linear.append(jnp.where(held, spectra[f, c], 0.0))
    for g in range(groups):
        block = jnp.stack([v[g * radii : (g + 1) * radii] for v in linear], axis=0)
        right[g * radii : (g + 1) * radii] = jnp.swapaxes(block, 0, 1)

    at = lax.broadcasted_iota(jnp.int32, (points, slots), 0)
    for f in range(4):
        log_here = log_rho[2 * f : 2 * f + 1]
        rise[f] = jnp.exp(log_here * (at + 1).astype(jnp.float32))
        fall[f] = jnp.exp(log_here * (points - at).astype(jnp.float32))

    before = (row * points).astype(jnp.float32)
    after = ((rows_count - 1 - row) * points).astype(jnp.float32)

    zero = jnp.zeros((radii, 128), jnp.float32)
    for q in range(12):
        states[3 * orders, q] = zero
    for c in range(chunks):
        for h in range(halves):
            piece(2, c, h).wait()
        turned_table[c] = analysis[c].T
    table_copy.wait()

    @pl.when(me == 0)
    def _():
        pl.semaphore_wait(planes_sem, rows_count - 1)
        for e in range(1, n):
            tell(rows_sem, ma=e)

    def chunk_step(c, carry):
        def unpack(k, carry):
            g = target(k)

            @pl.when(k > 0)
            def _():
                grid_copy(g, g, c).wait_recv()

            block = x[c, g].astype(jnp.float32).reshape(2, 6, 2, radii, 128)
            for j in range(2):
                at_order = 2 * g + j
                u_t, u_p, s_t, s_p, b_t, b_p = (block[j, q] for q in range(6))
                for q, (p, t) in enumerate(((b_p, b_t), (u_p, u_t), (s_p, s_t))):
                    plus = (p[0] - t[1], p[1] + t[0])
                    minus = (p[0] + t[1], p[1] - t[0])
                    parts = (plus[0], plus[1], minus[0], minus[1])
                    turned = (minus[0], -minus[1], plus[0], -plus[1])
                    for i in range(4):
                        states[at_order, 4 * q + i] = parts[i]
                        states[orders + at_order, 4 * q + i] = turned[i]
                        states[2 * orders + at_order, 4 * q + i] = 0.5 * parts[i]
            return carry

        lax.fori_loop(0, n, unpack, 0)

        def one_order(i, carry):
            e = served(i // 2)
            j = lax.rem(i, 2)
            t = 2 * e + j

            def add(a, total):
                b = partner[t, a]
                vp, vm, yp, ym, wp, wm = (
                    (states[a, 2 * q], states[a, 2 * q + 1], states[b, 2 * q], states[b, 2 * q + 1])
                    for q in range(6)
                )

                def square(v):
                    ar, ai, br, bi = v
                    return ar * br - ai * bi, ar * bi + ai * br

                def cross(v, w):
                    ar, ai, br, bi = v
                    cr, ci, dr, di = w
                    return (
                        (ar * dr - ai * di) + (cr * br - ci * bi),
                        (ar * di + ai * dr) + (cr * bi + ci * br),
                    )

                terms = []
                for v, y in ((vp, yp), (vm, ym)):
                    first_term, second_term = square(v), square(y)
                    terms += [first_term[0] - second_term[0], first_term[1] - second_term[1]]
                heat, other = cross(ym, wp), cross(yp, wm)
                terms += [heat[0] + other[0], heat[1] + other[1]]
                bent, other = cross(ym, vp), cross(yp, vm)
                terms += [bent[0] - other[0], bent[1] - other[1]]
                return tuple(v + w for v, w in zip(total, terms))

            pr, pi, mr, mi, hr, hi, er, ei = lax.fori_loop(0, orders, add, (zero,) * 8, unroll=8)
            rows = [pi - mi, mr - pr, pr + mr, pi + mi, -hr, -hi, ei, -er]
            block = jnp.swapaxes(jnp.stack(rows, axis=0), 0, 1).reshape(8 * radii, 128)
            block = (0.5 * block).astype(jnp.bfloat16)
            sums[c, e, pl.ds(pl.multiple_of(j * 8 * radii, 8 * radii), 8 * radii), :] = block

            @pl.when(jnp.logical_and(j == 1, e != me))
            def _():
                back_copy(e, me, c).start()

            return carry

        lax.fori_loop(0, orders, one_order, 0)
        got[c, me] = sums[c, me]
        return carry

    lax.fori_loop(0, chunks, chunk_step, 0)

    def project(c):
        for k in range(1, n):
            e = lax.rem(me + k, n)
            back_copy(e, e, c).wait_recv()
        terms = []
        for g in range(groups):
            lhs = jnp.concatenate([got[c, g * halves + h] for h in range(halves)], axis=1)
            total = jnp.dot(lhs, turned_table[c], preferred_element_type=jnp.float32)
            total = total.reshape(2, radii, 8, slots)
            terms.append(jnp.where(first, total[0], total[1]))
        return terms

    early = chunks - 1
    if early:
        for c in range(early):
            for k in range(1, n):
                e = lax.rem(me + k, n)
                back_copy(e, e, c).wait_recv()
        table = turned_table[0:early].reshape(early * halves * 128, slots)
        for g in range(groups):
            lhs = jnp.concatenate(
                [got[c, g * halves + h] for c in range(early) for h in range(halves)], axis=1
            )
            total = jnp.dot(lhs, table, preferred_element_type=jnp.float32)
            total = total.reshape(2, radii, 8, slots)
            right[g * radii : (g + 1) * radii] += jnp.where(first, total[0], total[1])
    terms = project(chunks - 1)
    source = [right[k] + terms[k // radii][k % radii] for k in range(points)]
    up, down = source[0], source[points - 1]
    ahead[0] = up
    back[points - 1] = down
    for k in range(1, points):
        up = source[k] + rho * up
        down = source[points - 1 - k] + rho * down
        ahead[k] = up
        back[points - 1 - k] = down
    @pl.when(me > 0)
    def _():
        pl.semaphore_wait(rows_sem, 1)

    edges[row] = jnp.concatenate([up, down], axis=0).astype(jnp.bfloat16)

    def edge_copy(e, source):
        return pltpu.make_async_remote_copy(
            src_ref=edges.at[row], dst_ref=edges.at[source],
            send_sem=edge_send.at[e], recv_sem=edge_recv.at[source],
            device_id={"row": e}, device_id_type=MESH,
        )

    for k in range(1, rows_count):
        edge_copy(lax.rem(row + k, rows_count), row).start()

    for g in range(groups):
        values = []
        for k in range(g * radii, (g + 1) * radii):
            value = ahead[k] + rho * back[k + 1] if k < points - 1 else ahead[k]
            values.append(inner * value)
        local_out[:, g * radii : (g + 1) * radii] = jnp.swapaxes(jnp.stack(values, axis=0), 0, 1)

    span = power(float(all_points + 1))
    scale = 1.0 / (1.0 - span * span)
    to_start, to_end = power(before), power(after)
    shifts = [power(float(k * points)) for k in range(rows_count)]
    zero = jnp.zeros((8, slots), jnp.float32)
    weights, reverses = [], []
    for e in range(rows_count):
        weight, reverse = zero, zero
        for k in range(rows_count - 1):
            weight = jnp.where(row - 1 - e == k, shifts[k], weight)
            reverse = jnp.where(e - row - 1 == k, shifts[k], reverse)
        weights.append(weight)
        reverses.append(reverse)

    for c in range(chunks):
        for k in range(1, n):
            e = lax.rem(me + k, n)
            grid_copy(e, e, c).wait_send()
            back_copy(e, e, c).wait_send()
    for k in range(1, rows_count):
        e = lax.rem(row + k, rows_count)
        edge_copy(e, e).wait()

    ahead_in, back_in, ahead_all, back_all = zero, zero, zero, zero
    for e in range(rows_count):
        both = edges[e].astype(jnp.float32)
        f_e, g_e = both[0:8], both[8:16]
        ahead_in += weights[e] * f_e
        back_in += reverses[e] * g_e
        ahead_all += shifts[rows_count - 1 - e] * f_e
        back_all += shifts[e] * g_e
    low = inner * rho * back_all
    high = inner * rho * ahead_all
    ends_out[0] = inner * ahead_in + (span * high - low) * scale * to_start
    ends_out[1] = inner * back_in + (span * low - high) * scale * to_end


def finish_kernel(inside, ends, rise, fall, out, result, sem):
    copies = []
    for q in range(8):
        left, right = ends[0, q : q + 1], ends[1, q : q + 1]
        result[q] = inside[q] + left * rise[q // 2] + right * fall[q // 2]
        copies.append(pltpu.make_async_copy(result.at[q], out.at[q], sem.at[q]))
        copies[-1].start()
    for copy in copies:
        copy.wait()


def local(n, rows_count, spectra, dtheta, dphi, analysis, pair_index, diffusivity):
    points, slots = spectra.shape[2], spectra.shape[3]
    radii = RADII
    halves = n * radii // points
    width = -(-dtheta.shape[1] // (128 * halves)) * 128
    extra = width * halves - dtheta.shape[1]
    if extra:
        dtheta, dphi, analysis = (jnp.pad(v, ((0, 0), (0, extra))) for v in (dtheta, dphi, analysis))
    chunks = width // 128
    vmem = pl.BlockSpec(memory_space=pltpu.VMEM)
    hbm = pl.BlockSpec(memory_space=pltpu.HBM)
    shape = spectra.shape
    table = pltpu.VMEM((chunks, slots, halves * 128), jnp.bfloat16)
    turned = pltpu.VMEM((points, 8, slots), jnp.float32)
    inside, ends, rise, fall = pl.pallas_call(
        functools.partial(step_kernel, n, rows_count),
        out_shape=(
            pltpu.VMEM((8, points, slots), jnp.float32),
            pltpu.VMEM((2, 8, slots), jnp.float32),
            pltpu.VMEM((4, points, slots), jnp.float32),
            pltpu.VMEM((4, points, slots), jnp.float32),
        ),
        in_specs=[hbm] * 6,
        out_specs=(vmem,) * 4,
        scratch_shapes=[
            pltpu.VMEM(shape, jnp.float32),
            table,
            table,
            table,
            pltpu.VMEM((chunks, halves * 128, slots), jnp.bfloat16),
            pltpu.VMEM((chunks, n, 24 * radii, 128), jnp.bfloat16),
            pltpu.VMEM((chunks, n, 24 * radii, 128), jnp.bfloat16),
            pltpu.VMEM((6 * n + 1, 12, radii, 128), jnp.float32),
            pltpu.VMEM((chunks, n, 16 * radii, 128), jnp.bfloat16),
            pltpu.VMEM((chunks, n, 16 * radii, 128), jnp.bfloat16),
            pltpu.VMEM((rows_count, 16, slots), jnp.bfloat16),
            turned,
            turned,
            turned,
            pltpu.VMEM((2 * n, 128), jnp.int32),
            pltpu.SMEM((2 * n, 128), jnp.int32),
            pltpu.SMEM(pair_index.shape, jnp.int32),
            pltpu.SMEM(diffusivity.shape, jnp.float32),
            pltpu.SemaphoreType.DMA((2 + points // radii,)),
            pltpu.SemaphoreType.DMA((3, chunks, halves)),
            pltpu.SemaphoreType.DMA((1,)),
            pltpu.SemaphoreType.DMA((chunks, n)),
            pltpu.SemaphoreType.DMA((chunks, n)),
            pltpu.SemaphoreType.DMA((chunks, n)),
            pltpu.SemaphoreType.DMA((chunks, n)),
            pltpu.SemaphoreType.DMA((rows_count,)),
            pltpu.SemaphoreType.DMA((rows_count,)),
            pltpu.SemaphoreType.REGULAR,
            pltpu.SemaphoreType.REGULAR,
            pltpu.SemaphoreType.REGULAR,
        ],
        compiler_params=pltpu.CompilerParams(
            collective_id=0, has_side_effects=True, vmem_limit_bytes=VMEM_LIMIT
        ),
        name="step",
    )(pair_index, diffusivity, spectra, dtheta, dphi, analysis)
    result = pl.pallas_call(
        finish_kernel,
        out_shape=jax.ShapeDtypeStruct((8, points, slots), jnp.float32),
        in_specs=[vmem] * 4,
        out_specs=hbm,
        scratch_shapes=[
            pltpu.VMEM((8, points, slots), jnp.float32), pltpu.SemaphoreType.DMA((8,))
        ],
        compiler_params=pltpu.CompilerParams(vmem_limit_bytes=8 * 1024 * 1024),
        name="finish",
    )(inside, ends, rise, fall)
    return result.reshape(shape)


def solution(mesh):
    n, rows_count = mesh.shape["ma"], mesh.shape["row"]
    return jax.shard_map(
        functools.partial(local, n, rows_count),
        mesh=mesh,
        in_specs=(
            P(None, None, "row", "ma"),
            P("ma", None),
            P("ma", None),
            P("ma", None),
            P(),
            P(),
        ),
        out_specs=P(None, None, "row", "ma"),
        check_vma=False,
    )
```
